128 devices in a mesh: row: 8 (over x_hi, z), col: 16 (over x_lo, y, core).
Axes of the slice: x: 4 (x_hi: 2, x_lo: 2; x = x_hi * 2 + x_lo), y: 4, z: 4, core: 2. Of those that a mesh axis runs over, the one named last changes fastest.
Arguments:
- inputs: bfloat16 [1024, 8192], P('col', 'row'), may hold values from -6 to 6
- out_grad: bfloat16 [1024, 8192], P('col', 'row'), may hold values from -0.375 to 0.375
- gate_pre: bfloat16 [1024, 28672], P('row', 'col'), may hold values from -8 to 8
- up_pre: bfloat16 [1024, 28672], P('row', 'col'), may hold values from -6 to 6
- gate_weight: bfloat16 [8192, 28672], P('row', 'col'), may hold values from -0.25 to 0.25
- up_weight: bfloat16 [8192, 28672], P('row', 'col'), may hold values from -0.25 to 0.25
- down_weight: bfloat16 [8192, 28672], P('row', 'col'), may hold values from -0.03125 to 0.03125
Outputs:
- input_grad: bfloat16 [1024, 8192], P('col', 'row')
- gate_weight_grad: bfloat16 [8192, 28672], P('row', 'col')
- up_weight_grad: bfloat16 [8192, 28672], P('row', 'col')
- down_weight_grad: bfloat16 [8192, 28672], P('row', 'col')
The draws below stay inside these ranges and needn't reach their ends.
All inputs are finite; a program needn't handle non-finite values.
Results may differ from the reference program's by a relative error of at most 0.0055.
Values may be sent and summed in bfloat16 or wider, within the bound.
A program may use at most 128 MiB of HBM per device.

```python
import jax
import jax.numpy as jnp
from jax import lax

D = 8192
FF = 28672
TOKENS = 1024


def levels(stream_key, dims, split, low, top_value):
    loudness, own = 1.0, jax.random.fold_in(stream_key, 6)
    for position, parts in split:
        steps = jnp.exp(jax.random.uniform(jax.random.fold_in(own, position), (parts,), jnp.float32, low / len(split), top_value / len(split)))
        loudness = loudness * jnp.repeat(steps, dims[position] // parts).reshape([-1 if axis == position else 1 for axis in range(len(dims))])
    return loudness


def gaussian(stream_key, dims, width, most, pieces=(), held_as=jnp.bfloat16):
    level = levels(stream_key, dims, pieces, -0.22, 0.18) if pieces else 1.0
    values = jax.random.normal(stream_key, dims, jnp.float32) * width * level
    return jnp.minimum(jnp.maximum(values, -most), most).astype(held_as)


def setup_inputs(seed: int = 0) -> dict:
    seeds = jax.random.split(jax.random.key(seed), 8)
    return {
        "inputs": gaussian(seeds[0], (TOKENS, D), 1.0, 6.0, ((0, 16), (1, 8))),
        "out_grad": gaussian(seeds[1], (TOKENS, D), (2.0 / TOKENS ** 0.5), 0.375, ((0, 16), (1, 8))),
        "gate_pre": gaussian(seeds[2], (TOKENS, FF), 1.5, 8.0, ((0, 8), (1, 16))),
        "up_pre": gaussian(seeds[3], (TOKENS, FF), 1.0, 6.0, ((0, 8), (1, 16))),
        "gate_weight": gaussian(seeds[4], (D, FF), (D // 16) ** -0.5, 0.25, ((0, 8), (1, 16))),
        "up_weight": gaussian(seeds[5], (D, FF), (D // 16) ** -0.5, 0.25, ((0, 8), (1, 16))),
        "down_weight": gaussian(seeds[6], (D, FF), FF ** -0.5, 0.03125, ((0, 8), (1, 16))),
    }


def reference(inputs, out_grad, gate_pre, up_pre, gate_weight, up_weight, down_weight):
    hidden_grad = jnp.dot(out_grad, down_weight, preferred_element_type=jnp.float32)
    gate_value = gate_pre.astype(jnp.float32)
    up_value = up_pre.astype(jnp.float32)
    sigmoid_gate = jax.nn.sigmoid(gate_value)
    activated = gate_value * sigmoid_gate
    gate_act_grad = (hidden_grad * up_value * sigmoid_gate * (1.0 + gate_value * (1.0 - sigmoid_gate))).astype(jnp.bfloat16)
    up_act_grad = (hidden_grad * activated).astype(jnp.bfloat16)
    hidden = (activated * up_value).astype(jnp.bfloat16)
    last_dims = (((1,), (1,)), ((), ()))
    first_dims = (((0,), (0,)), ((), ()))
    input_grad = (lax.dot_general(gate_act_grad, gate_weight, last_dims, preferred_element_type=jnp.float32)
                  + lax.dot_general(up_act_grad, up_weight, last_dims, preferred_element_type=jnp.float32)).astype(jnp.bfloat16)
    gate_weight_grad = lax.dot_general(inputs, gate_act_grad, first_dims, preferred_element_type=jnp.float32).astype(jnp.bfloat16)
    up_weight_grad = lax.dot_general(inputs, up_act_grad, first_dims, preferred_element_type=jnp.float32).astype(jnp.bfloat16)
    down_weight_grad = lax.dot_general(out_grad, hidden, first_dims, preferred_element_type=jnp.float32).astype(jnp.bfloat16)
    return input_grad, gate_weight_grad, up_weight_grad, down_weight_grad
```

```python
import functools

import jax
import jax.numpy as jnp
from jax import lax
from jax.experimental import pallas as pl
from jax.experimental.pallas import tpu as pltpu
from jax.sharding import PartitionSpec as P

BF = jnp.bfloat16
F32 = jnp.float32
NC = 4
N_MSG = 180


def comm_kernel(
    x_in, dy_in, g_in, u_in, wg_in, wu_in, wd_in,
    out, ga_out, ua_out, hi_out, xt_out, dyt_out,
    X, DY, G, U, WG, WU, WD, HP, RX, SZ, RZ, RF, H, GA, UA, HI, XT, DYT,
    IGP, RC, IS, RY, IX, RL,
    ssem, rsem, lsem,
):
    D = DY.shape[-1]
    F = G.shape[-1]
    row, col = lax.axis_index("row"), lax.axis_index("col")
    h, z = lax.div(row, 4), lax.rem(row, 4)
    xl, y, core = lax.div(col, 8), lax.rem(lax.div(col, 2), 4), lax.rem(col, 2)
    z1, z2, z3 = lax.rem(z + 1, 4), lax.rem(z + 2, 4), lax.rem(z + 3, 4)
    y1, y2, y3 = lax.rem(y + 1, 4), lax.rem(y + 2, 4), lax.rem(y + 3, 4)
    oh, oxl, oc = 1 - h, 1 - xl, 1 - core

    def rid(hh, zz):
        return hh * 4 + zz

    def cid(xx, yy, cc):
        return xx * 8 + yy * 2 + cc

    p_zp, p_zm, p_x = (rid(h, z1), col), (rid(h, z3), col), (rid(oh, z), col)
    p_yp, p_ym, p_y2 = (row, cid(xl, y1, core)), (row, cid(xl, y3, core)), (row, cid(xl, y2, core))
    p_xl, p_s = (row, cid(oxl, y, core)), (row, cid(xl, y, oc))

    n_msg = [0]
    n_loc = [0]
    sent = []
    local = []

    def send(src, dst, peer):
        i = n_msg[0]
        n_msg[0] += 1
        cp = pltpu.make_async_remote_copy(
            src_ref=src, dst_ref=dst, send_sem=ssem.at[i], recv_sem=rsem.at[i],
            device_id=peer, device_id_type=pl.DeviceIdType.MESH,
        )
        cp.start()
        sent.append(cp)
        return cp

    def load(src, dst):
        i = n_loc[0]
        n_loc[0] += 1
        cp = pltpu.make_async_copy(src, dst, lsem.at[i])
        cp.start()
        return cp

    def store(src, dst):
        local.append(load(src, dst))

    bar = pltpu.get_barrier_semaphore()
    peers = (p_zp, p_zm, p_x, p_yp, p_ym, p_y2, p_xl, p_s)
    for p in peers:
        pl.semaphore_signal(bar, inc=1, device_id=p, device_id_type=pl.DeviceIdType.MESH)
    pl.semaphore_wait(bar, len(peers))

    class ColGather:
        def __init__(self, B, src):
            self.B = B
            self.own = load(src, B.at[col])
            me = B.at[col]
            self.m_s = send(src, me, p_s)
            self.m_x = send(src, me, p_xl)
            self.m_y = [send(src, me, p) for p in (p_yp, p_ym, p_y2)]

        def s1(self):
            B = self.B
            self.m_x.wait_recv()
            b = B.at[cid(oxl, y, core)]
            self.m_p = [send(b, b, p) for p in (p_yp, p_ym, p_y2)]
            self.sib = [send(b, b, p_s)]

        def s2(self):
            B = self.B
            for m, yy in zip(self.m_y, (y3, y1, y2)):
                m.wait_recv()
                b = B.at[cid(xl, yy, core)]
                self.sib.append(send(b, b, p_s))

        def s3(self):
            B = self.B
            for m, yy in zip(self.m_p, (y3, y1, y2)):
                m.wait_recv()
                b = B.at[cid(oxl, yy, core)]
                self.sib.append(send(b, b, p_s))

        def done(self):
            self.own.wait()
            self.m_s.wait_recv()
            for m in self.sib:
                m.wait_recv()

    class RowGather:
        def __init__(self, B, n, mode, src=None):
            self.B, self.n, self.mode = B, n, mode
            me = self.blk(h, z)
            src = me if src is None else src
            self.m_zp = send(src, me, p_zp)
            self.m_zm = send(src, me, p_zm)
            self.m_x = send(src, me, p_x)

        def blk(self, hh, zz, lo=0, cnt=None):
            n = self.n
            return self.B.at[pl.ds(rid(hh, zz) * n + lo, n - lo if cnt is None else cnt)]

        def s1(self):
            n, q, blk = self.n, self.n // 2, self.blk
            self.m_zp.wait_recv()
            a = blk(h, z3, 0, q)
            self.m_fa = send(a, a, p_zp)
            self.m_zm.wait_recv()
            b = blk(h, z1, q, q)
            self.m_fb = send(b, b, p_zm)
            self.k1 = {"x": n, "z": 0, "m": q}[self.mode]
            if self.k1 < n:
                lo, cnt = self.k1, n - self.k1
                a = blk(h, z3, lo, cnt)
                self.m_xa = send(a, a, p_x)
                b = blk(h, z1, lo, cnt)
                self.m_xb = send(b, b, p_x)

        def s1b(self):
            self.m_x.wait_recv()
            if self.k1:
                a = self.blk(oh, z, 0, self.k1)
                self.m_pp = send(a, a, p_zp)
                self.m_pm = send(a, a, p_zm)

        def s2(self):
            blk, k1 = self.blk, self.k1
            if k1:
                q = k1 // 2
                self.m_pp.wait_recv()
                a = blk(oh, z3, 0, q)
                self.m_pfa = send(a, a, p_zp)
                self.m_pm.wait_recv()
                b = blk(oh, z1, q, q)
                self.m_pfb = send(b, b, p_zm)

        def s2b(self):
            self.m_fa.wait_recv()
            self.m_fb.wait_recv()
            if self.k1 < self.n:
                a = self.blk(h, z2, self.k1, self.n - self.k1)
                self.m_xc = send(a, a, p_x)

        def done(self):
            if self.k1:
                self.m_pfa.wait_recv()
                self.m_pfb.wait_recv()
            if self.k1 < self.n:
                self.m_xa.wait_recv()
                self.m_xb.wait_recv()
                self.m_xc.wait_recv()

    dyg = ColGather(DY, dy_in)
    ld_wd = load(wd_in, WD)
    gg = RowGather(G, 4, "x", g_in)
    own_g = load(g_in, gg.blk(h, z))
    ug = RowGather(U, 4, "m", u_in)
    own_u = load(u_in, ug.blk(h, z))
    ld_wg = load(wg_in, WG)
    ld_wu = load(wu_in, WU)
    dyg.s1()
    dyg.s2()
    dyg.s3()
    xg = ColGather(X, x_in)
    dyg.done()
    ld_wd.wait()

    ft = 256 if F % 256 == 0 else 128
    dt = 256 if D % 256 == 0 else 128

    m_rx = []

    def mm_h(c):
        a = DY[:, 16 * c:16 * c + 16, :].reshape(256, D)

        def body(n, _):
            s = pl.ds(pl.multiple_of(n * ft, ft), ft)
            HP[c, :, :, s] = jnp.dot(a, WD[:, s], preferred_element_type=F32).astype(BF).reshape(16, 16, ft)
            return 0

        lax.fori_loop(0, F // ft, body, 0)
        m_rx.append(send(HP.at[c, pl.ds(8 * oh, 8)], RX.at[c], p_x))

    def own_sum(c, zz, k):
        return HP[c, 8 * h + 2 * zz + k].astype(F32) + RX[c, 2 * zz + k].astype(F32)

    m_rz, m_rf, hg = {}, {}, {}

    def st_a(c):
        m_rx[c].wait_recv()
        SZ[c, 0, 0] = own_sum(c, z2, 0).astype(BF)
        a = send(SZ.at[c, 0, 0], RZ.at[c, 0], p_zm)
        SZ[c, 0, 1] = own_sum(c, z2, 1).astype(BF)
        b = send(SZ.at[c, 0, 1], RZ.at[c, 1], p_zp)
        m_rz[c] = (a, b)
        SZ[c, 1, 0] = own_sum(c, z1, 0).astype(BF)
        p0 = send(SZ.at[c, 1, 0], RF.at[c, 0, 0], p_zp)
        SZ[c, 2, 1] = own_sum(c, z3, 1).astype(BF)
        q1 = send(SZ.at[c, 2, 1], RF.at[c, 1, 1], p_zm)
        m_rf[c] = [p0, q1]

    def st_b(c):
        a, b = m_rz[c]
        b.wait_recv()
        SZ[c, 1, 1] = (own_sum(c, z1, 1) + RZ[c, 1].astype(F32)).astype(BF)
        m_rf[c].append(send(SZ.at[c, 1, 1], RF.at[c, 0, 1], p_zp))
        a.wait_recv()
        SZ[c, 2, 0] = (own_sum(c, z3, 0) + RZ[c, 0].astype(F32)).astype(BF)
        m_rf[c].append(send(SZ.at[c, 2, 0], RF.at[c, 1, 0], p_zm))

    def st_c(c):
        for m in m_rf[c]:
            m.wait_recv()
        for k in range(2):
            H[c, 2 * row + k] = (
                own_sum(c, z, k) + RF[c, 0, k].astype(F32) + RF[c, 1, k].astype(F32)
            ).astype(BF)
        hg[c] = RowGather(H.at[c], 2, "x")

    def st_f(c):
        hg[c].done()
        rows = pl.ds(16 * (c % 2), 16)

        def body(j, _):
            g = G[2 * j + c // 2, rows].astype(F32)
            u = U[2 * j + c // 2, rows].astype(F32)
            hh = H[c, j].astype(F32)
            s = 1.0 / (1.0 + jnp.exp(-g))
            act = g * s
            GA[j, 16 * c:16 * c + 16] = (hh * u * s * (1.0 + g * (1.0 - s))).astype(BF)
            UA[j, 16 * c:16 * c + 16] = (hh * act).astype(BF)
            HI[j, 16 * c:16 * c + 16] = (act * u).astype(BF)
            return 0

        lax.fori_loop(0, 16, body, 0)
        for src, dst in ((GA, ga_out), (UA, ua_out), (HI, hi_out)):
            store(src.at[:, pl.ds(16 * c, 16)], dst.at[:, pl.ds(16 * c, 16)])

    m_c, m_y, m_l = {}, {}, {}

    def st_g(c):
        a = GA[:, 16 * c:16 * c + 16, :].reshape(256, F)
        b = UA[:, 16 * c:16 * c + 16, :].reshape(256, F)
        dims = (((1,), (1,)), ((), ()))

        def body(n, _):
            s = pl.ds(pl.multiple_of(n * dt, dt), dt)
            v = lax.dot_general(a, WG[s, :], dims, preferred_element_type=F32)
            v += lax.dot_general(b, WU[s, :], dims, preferred_element_type=F32)
            IGP[c, :, :, :, s] = v.reshape(8, 2, 16, dt)
            return 0

        lax.fori_loop(0, D // dt, body, 0)
        m_c[c] = send(IGP.at[c, :, oc], RC.at[c], p_s)

    def st_i(c):
        m_c[c].wait_recv()
        for xx in range(2):
            for yy in range(4):
                m = xx * 4 + yy
                IS[c, yy, xx] = (IGP[c, m, core] + RC[c, m]).astype(BF)
        m_y[c] = [
            send(IS.at[c, yy], RY.at[c, i], p)
            for i, (yy, p) in enumerate(((y1, p_yp), (y3, p_ym), (y2, p_y2)))
        ]

    def y_sum(c, xx):
        v = IS[c, y, xx].astype(F32)
        for i in range(3):
            v += RY[c, i, xx].astype(F32)
        return v

    def st_j(c):
        for m in m_y[c]:
            m.wait_recv()
        IX[c] = y_sum(c, oxl)
        m_l[c] = send(IX.at[c], RL.at[c], p_xl)

    def st_k(c):
        m_l[c].wait_recv()
        out[16 * c:16 * c + 16, :] = (y_sum(c, xl) + RL[c]).astype(BF)

    def transpose(B, T, dst):
        def body(r, _):
            v = B[pl.ds(2 * r, 2)].reshape(128, D)
            T[:, pl.ds(pl.multiple_of(r * 128, 128), 128)] = v.T
            return 0

        lax.fori_loop(0, 8, body, 0)
        store(T, dst)

    def finish_pre():
        own_g.wait()
        own_u.wait()
        gg.done()
        ug.done()
        ld_wg.wait()
        ld_wu.wait()

    def finish_x():
        xg.done()
        transpose(X, XT, xt_out)

    steps = [
        (14, lambda: mm_h(0)), (16, lambda: mm_h(1)), (18, gg.s1), (18.5, gg.s1b),
        (19, lambda: mm_h(2)), (21, lambda: mm_h(3)), (22, xg.s1), (23, ug.s1), (23.5, ug.s1b),
        (24, xg.s2), (25, lambda: transpose(DY, DYT, dyt_out)), (31, xg.s3), (33, finish_x),
        (40, gg.s2), (40.5, gg.s2b), (45, ug.s2), (45.5, ug.s2b), (50, finish_pre),
    ]
    base = {"a": 30, "b": 34, "c": 38, "d": 44, "e": 50, "f": 56, "g": 57, "i": 60, "j": 65, "k": 70}
    fns = {
        "a": st_a, "b": st_b, "c": st_c,
        "d": lambda c: (hg[c].s1(), hg[c].s1b()), "e": lambda c: (hg[c].s2(), hg[c].s2b()),
        "f": st_f, "g": st_g, "i": st_i, "j": st_j, "k": st_k,
    }
    for name, t in base.items():
        for c in range(NC):
            steps.append((t + 10 * c, functools.partial(fns[name], c)))
    for _, fn in sorted(steps, key=lambda s: s[0]):
        fn()

    for cp in sent:
        cp.wait_send()
    for cp in local:
        cp.wait()


def grads_kernel(xt, dyt, ga, ua, hi, og, ou, od):
    og[...] = jnp.dot(xt[...], ga[...], preferred_element_type=F32).astype(BF)
    ou[...] = jnp.dot(xt[...], ua[...], preferred_element_type=F32).astype(BF)
    od[...] = jnp.dot(dyt[...], hi[...], preferred_element_type=F32).astype(BF)


def on_device(inputs, out_grad, gate_pre, up_pre, gate_weight, up_weight, down_weight):
    D, F = gate_weight.shape
    T = 1024
    any_spec = pl.BlockSpec(memory_space=pl.ANY)
    v = pltpu.VMEM
    scratch = [
        v((16, 64, D), BF), v((16, 64, D), BF),
        v((32, 32, F), BF), v((32, 32, F), BF),
        v((D, F), BF), v((D, F), BF), v((D, F), BF),
        v((NC, 16, 16, F), BF), v((NC, 8, 16, F), BF),
        v((NC, 3, 2, 16, F), BF), v((NC, 2, 16, F), BF), v((NC, 2, 2, 16, F), BF),
        v((NC, 16, 16, F), BF),
        v((16, 64, F), BF), v((16, 64, F), BF), v((16, 64, F), BF),
        v((D, T), BF), v((D, T), BF),
        v((NC, 8, 2, 16, D), F32), v((NC, 8, 16, D), F32),
        v((NC, 4, 2, 16, D), BF), v((NC, 3, 2, 16, D), BF),
        v((NC, 16, D), F32), v((NC, 16, D), F32),
        pltpu.SemaphoreType.DMA((N_MSG,)), pltpu.SemaphoreType.DMA((N_MSG,)), pltpu.SemaphoreType.DMA((32,)),
    ]
    sd = jax.ShapeDtypeStruct
    input_grad, ga, ua, hi, xt, dyt = pl.pallas_call(
        comm_kernel,
        out_shape=(
            sd((64, D), BF), sd((16, 64, F), BF), sd((16, 64, F), BF), sd((16, 64, F), BF),
            sd((D, T), BF), sd((D, T), BF),
        ),
        in_specs=[any_spec] * 7,
        out_specs=(pl.BlockSpec(memory_space=pltpu.VMEM),) + (any_spec,) * 5,
        scratch_shapes=scratch,
        compiler_params=pltpu.CompilerParams(
            collective_id=0, has_side_effects=True, vmem_limit_bytes=62 << 20
        ),
        cost_estimate=pl.CostEstimate(flops=12 * D * F * T // 2, bytes_accessed=30 << 20, transcendentals=T * F),
        name="comm",
    )(
        inputs, out_grad, gate_pre.reshape(4, 32, F), up_pre.reshape(4, 32, F),
        gate_weight, up_weight, down_weight,
    )
    ft = 256 if F % 256 == 0 else 128
    full = pl.BlockSpec((D, T), lambda n: (0, 0))
    tile = pl.BlockSpec((T, ft), lambda n: (0, n))
    otile = pl.BlockSpec((D, ft), lambda n: (0, n))
    gw, uw, dw = pl.pallas_call(
        grads_kernel,
        grid=(F // ft,),
        out_shape=(sd((D, F), BF),) * 3,
        in_specs=[full, full, tile, tile, tile],
        out_specs=(otile,) * 3,
        compiler_params=pltpu.CompilerParams(vmem_limit_bytes=48 << 20),
        cost_estimate=pl.CostEstimate(flops=6 * D * F * T, bytes_accessed=26 << 20, transcendentals=0),
        name="weight_grads",
    )(xt, dyt, ga.reshape(T, F), ua.reshape(T, F), hi.reshape(T, F))
    return input_grad, gw, uw, dw


def solution(mesh):
    in_specs = (P("col", "row"), P("col", "row")) + (P("row", "col"),) * 5
    out_specs = (P("col", "row"), P("row", "col"), P("row", "col"), P("row", "col"))
    return jax.shard_map(
        on_device, mesh=mesh, in_specs=in_specs, out_specs=out_specs, check_vma=False
    )
```

```python
import jax
import jax.numpy as jnp
from jax import lax
from jax.experimental import pallas as pl
from jax.experimental.pallas import tpu as pltpu
from jax.sharding import PartitionSpec as P

BF = jnp.bfloat16
F32 = jnp.float32
NC = 4
N_MSG = 180
VMEM_LIMIT = 63 << 20
K1_G, K1_U, K1_H = 8, 6, (2, 2, 2, 0)

ORDER = [
    "u0", "dy0", "dyfym", "g0", "dy1", "dyfyp", "dyfy2", "dyfpp", "dyfp2", "wd", "dyfpm", "u1a", "u1b", "h0m",
    "wgu", "g1c", "u1c", "h3m", "h2m", "g2a", "h0a", "g2b", "h1m", "g1a", "g1b", "h0b1", "h0b0", "u2c", "h3a",
    "h00", "h3b0", "tdy", "h3b1", "h2a", "h30", "u2b", "h2b0", "u2a", "h31a", "h2b1", "h31b", "h1a", "down0",
    "h01c", "down1", "h20", "down2", "down3", "h32c", "h1b1", "x0", "h1b0", "h02b", "h02a", "h01b", "h01a",
    "h21c", "h10", "x1", "h21b", "h21a", "h0f", "h3f", "h3g", "h22a", "h22b", "h11c", "h0g", "h2f", "h3i",
    "h11a", "h11b", "h0i", "h12a", "h12b", "h2g", "h1f", "h1g", "h2i", "xfym", "xfp2", "h0j", "xfpm", "h1i",
    "xfyp", "down4", "xfpp", "h3j", "down5", "h2j", "down6", "h0k", "h1j", "xfy2", "h3k", "tx", "h2k", "h1k",
]


def run_steps(steps, wait):
    assert sorted(ORDER) == sorted(steps)
    for name in ORDER:
        msgs, _, fn = steps[name]
        for m in msgs:
            wait(m)
        fn()


def comm_kernel(
    x_in, dy_in, g_in, u_in, wg_in, wu_in, wd_in,
    out, ga_out, ua_out, xt_out, dw_out,
    X, DY, G, U, WG, WU, WD, HP, RX, SZ, RZ, RF, H, GA, UA, HT, XT, DYT,
    IGP, RC, IS, RY, IX, RL,
    ssem, rsem, lsem,
):
    D = DY.shape[-1]
    F = G.shape[-1]
    row, col = lax.axis_index("row"), lax.axis_index("col")
    h, z = lax.div(row, 4), lax.rem(row, 4)
    xl, y, core = lax.div(col, 8), lax.rem(lax.div(col, 2), 4), lax.rem(col, 2)
    z1, z2, z3 = lax.rem(z + 1, 4), lax.rem(z + 2, 4), lax.rem(z + 3, 4)
    y1, y2, y3 = lax.rem(y + 1, 4), lax.rem(y + 2, 4), lax.rem(y + 3, 4)
    oh, oxl, oc = 1 - h, 1 - xl, 1 - core

    def rid(hh, zz):
        return hh * 4 + zz

    def cid(xx, yy, cc):
        return xx * 8 + yy * 2 + cc

    p_zp, p_zm, p_x = (rid(h, z1), col), (rid(h, z3), col), (rid(oh, z), col)
    p_yp, p_ym, p_y2 = (row, cid(xl, y1, core)), (row, cid(xl, y3, core)), (row, cid(xl, y2, core))
    p_xl, p_s = (row, cid(oxl, y, core)), (row, cid(xl, y, oc))

    msgs = {}
    waited = set()
    left = set()
    loads = {}
    stores = []
    steps = {}

    def send(name, src, dst, peer):
        i = len(msgs)
        msgs[name] = pltpu.make_async_remote_copy(
            src_ref=src, dst_ref=dst, send_sem=ssem.at[i], recv_sem=rsem.at[i],
            device_id=peer, device_id_type=pl.DeviceIdType.MESH,
        )
        msgs[name].start()

    def wait(name):
        if name in waited:
            return
        waited.add(name)
        if name in loads:
            loads[name].wait()
        else:
            msgs[name].wait_recv()

    def wait_send(name):
        if name not in left:
            left.add(name)
            msgs[name].wait_send()

    def copy(src, dst):
        cp = pltpu.make_async_copy(src, dst, lsem.at[len(loads) + len(stores)])
        cp.start()
        return cp

    def load(name, src, dst):
        loads[name] = copy(src, dst)

    def store(src, dst):
        stores.append(copy(src, dst))

    def step(name, waits, after, fn):
        steps[name] = (waits, after, fn)

    bar = pltpu.get_barrier_semaphore()
    peers = (p_zp, p_zm, p_x, p_yp, p_ym, p_y2, p_xl, p_s)
    for p in peers:
        pl.semaphore_signal(bar, inc=1, device_id=p, device_id_type=pl.DeviceIdType.MESH)
    pl.semaphore_wait(bar, len(peers))

    def col_gather(nm, B, src):
        own = B.at[col]

        def s0():
            for k, p in (("x", p_xl), ("yp", p_yp), ("ym", p_ym), ("y2", p_y2), ("s", p_s)):
                send(nm + k, src, own, p)
            load(nm + "own", src, own)

        def s1():
            b = B.at[cid(oxl, y, core)]
            for k, p in (("pp", p_yp), ("pm", p_ym), ("p2", p_y2), ("sx", p_s)):
                send(nm + k, b, b, p)

        def fwd(k, xx, yy):
            b = B.at[cid(xx, yy, core)]
            step(nm + "f" + k, [nm + k], [], lambda: send(nm + "s" + k, b, b, p_s))

        step(nm + "0", [], [], s0)
        step(nm + "1", [nm + "x"], [], s1)
        for k, yy in (("p", y3), ("m", y1), ("2", y2)):
            fwd("y" + k, xl, yy)
            fwd("p" + k, oxl, yy)
        return [nm + k for k in ("own", "s", "sx", "syp", "sym", "sy2", "spp", "spm", "sp2")]

    def row_gather(nm, B, n, k1, src=None, first=None, after=()):
        q, kq = n // 2, k1 // 2

        def blk(hh, zz, lo=0, cnt=n):
            return B.at[pl.ds(rid(hh, zz) * n + lo, cnt)]

        def fw(k, p, *b):
            send(nm + k, blk(*b), blk(*b), p)

        def s0():
            if first is not None:
                first()
            me = blk(h, z)
            for k, p in (("x", p_x), ("zp", p_zp), ("zm", p_zm)):
                send(nm + k, me if src is None else src, me, p)
            if src is not None:
                load(nm + "own", src, me)

        def s1a():
            fw("fa", p_zp, h, z3, 0, q)
            if k1 < n:
                fw("xa", p_x, h, z3, k1, n - k1)

        def s1b():
            fw("fb", p_zm, h, z1, q, q)
            if k1 < n:
                fw("xb", p_x, h, z1, k1, n - k1)

        def s1c():
            fw("pp", p_zp, oh, z, 0, k1)
            fw("pm", p_zm, oh, z, 0, k1)

        step(nm + "0", after[0] if after else [], after[1] if after else [], s0)
        step(nm + "1a", [nm + "zp"], [], s1a)
        step(nm + "1b", [nm + "zm"], [], s1b)
        ends = [nm + "x", nm + "fa", nm + "fb"] + ([] if src is None else [nm + "own"])
        if k1:
            step(nm + "1c", [nm + "x"], [], s1c)
            step(nm + "2a", [nm + "pp"], [], lambda: fw("pfa", p_zp, oh, z3, 0, kq))
            step(nm + "2b", [nm + "pm"], [], lambda: fw("pfb", p_zm, oh, z1, kq, kq))
            ends += [nm + "pfa", nm + "pfb"]
        if k1 < n:
            need = [nm + "fb"] + ([nm + "fa"] if k1 < q else [])
            step(nm + "2c", need, [], lambda: fw("xc", p_x, h, z2, k1, n - k1))
            ends += [nm + "xa", nm + "xb", nm + "xc"]
        return ends

    dy_ends = col_gather("dy", DY, dy_in)
    x_ends = col_gather("x", X, x_in)
    g_ends = row_gather("g", G, 8, K1_G, g_in)
    u_ends = row_gather("u", U, 8, K1_U, u_in)
    step("wd", [], [], lambda: load("wd", wd_in, WD))
    step("wgu", [], [], lambda: (load("wg", wg_in, WG), load("wu", wu_in, WU)))

    def t_x():
        def body(r, _):
            for c in range(NC):
                v = X[pl.ds(8 * r, 8), 16 * c:16 * c + 16, :].reshape(128, D)
                XT[:, pl.ds(pl.multiple_of(256 * c + r * 128, 128), 128)] = v.T
            return 0

        lax.fori_loop(0, 2, body, 0)
        store(XT, xt_out)

    def t_dy():
        def body(r, _):
            DYT[:, pl.ds(pl.multiple_of(r * 128, 128), 128)] = DY[pl.ds(2 * r, 2)].reshape(128, D).T
            return 0

        lax.fori_loop(0, 8, body, 0)

    step("tx", x_ends, [], t_x)
    step("tdy", dy_ends, [], t_dy)

    gu_ends = g_ends + u_ends
    n_down = 7 if F % 7 == 0 else 1
    fd = F // n_down

    def down_part(n):
        s = slice(fd * n, fd * (n + 1))

        def body(j, _):
            g = G[pl.ds(8 * j, 8), :, s].astype(F32)
            act = g * (0.5 * jnp.tanh(0.5 * g) + 0.5)
            v = (act * U[pl.ds(8 * j, 8), :, s].astype(F32)).astype(BF)
            HT[pl.ds(2 * j, 2)] = v.reshape(2, 64, fd)
            return 0

        lax.fori_loop(0, 8, body, 0)
        WD[:, s] = jnp.dot(DYT[...], HT[...].reshape(1024, fd), preferred_element_type=F32).astype(BF)
        if n == n_down - 1:
            store(WD, dw_out)

    for n in range(n_down):
        before = [f"down{n - 1}"] if n else ["tdy"] + [f"h{c}m" for c in range(NC)]
        step(f"down{n}", gu_ends, before, lambda n=n: down_part(n))

    def chunk(c):
        nm = f"h{c}"

        def mm_h():
            a = DY[:, 16 * c:16 * c + 16, :].reshape(256, D)
            HP[c] = jnp.dot(a, WD[...], preferred_element_type=F32).astype(BF).reshape(16, 16, F)
            send(nm + "rx", HP.at[c, pl.ds(8 * oh, 8)], RX.at[c], p_x)

        def own_sum(zz, k):
            return HP[c, 8 * h + 2 * zz + k].astype(F32) + RX[c, 2 * zz + k].astype(F32)

        def st_a():
            SZ[c, 0, 0] = own_sum(z2, 0).astype(BF)
            send(nm + "rz0", SZ.at[c, 0, 0], RZ.at[c, 0], p_zm)
            SZ[c, 0, 1] = own_sum(z2, 1).astype(BF)
            send(nm + "rz1", SZ.at[c, 0, 1], RZ.at[c, 1], p_zp)
            SZ[c, 1, 0] = own_sum(z1, 0).astype(BF)
            send(nm + "rf00", SZ.at[c, 1, 0], RF.at[c, 0, 0], p_zp)
            SZ[c, 2, 1] = own_sum(z3, 1).astype(BF)
            send(nm + "rf11", SZ.at[c, 2, 1], RF.at[c, 1, 1], p_zm)

        def st_b1():
            SZ[c, 1, 1] = (own_sum(z1, 1) + RZ[c, 1].astype(F32)).astype(BF)
            send(nm + "rf01", SZ.at[c, 1, 1], RF.at[c, 0, 1], p_zp)

        def st_b0():
            SZ[c, 2, 0] = (own_sum(z3, 0) + RZ[c, 0].astype(F32)).astype(BF)
            send(nm + "rf10", SZ.at[c, 2, 0], RF.at[c, 1, 0], p_zm)

        def st_c():
            for k in range(2):
                H[c, 2 * row + k] = (
                    own_sum(z, k) + RF[c, 0, k].astype(F32) + RF[c, 1, k].astype(F32)
                ).astype(BF)

        def st_f():
            def body(j, _):
                g = G[4 * j + c].astype(F32)
                u = U[4 * j + c].astype(F32)
                hh = H[c, j].astype(F32)
                s = 0.5 * jnp.tanh(0.5 * g) + 0.5
                GA[c, j] = (hh * u * s * (1.0 + g * (1.0 - s))).astype(BF)
                UA[c, j] = (hh * g * s).astype(BF)
                return 0

            lax.fori_loop(0, 16, body, 0)
            store(GA.at[c], ga_out.at[c])
            store(UA.at[c], ua_out.at[c])

        def st_g():
            dims = (((1,), (1,)), ((), ()))
            v = lax.dot_general(GA[c].reshape(256, F), WG[...], dims, preferred_element_type=F32)
            v += lax.dot_general(UA[c].reshape(256, F), WU[...], dims, preferred_element_type=F32)
            IGP[c] = v.reshape(8, 2, 16, D)
            send(nm + "c", IGP.at[c, :, oc], RC.at[c], p_s)

        def st_i():
            for xx in range(2):
                for yy in range(4):
                    m = xx * 4 + yy
                    IS[c, yy, xx] = (IGP[c, m, core] + RC[c, m]).astype(BF)
            for i, (yy, p) in enumerate(((y1, p_yp), (y3, p_ym), (y2, p_y2))):
                send(nm + f"y{i}", IS.at[c, yy], RY.at[c, i], p)

        def y_sum(xx):
            v = IS[c, y, xx].astype(F32)
            for i in range(3):
                v += RY[c, i, xx].astype(F32)
            return v

        def st_j():
            IX[c] = y_sum(oxl)
            send(nm + "l", IX.at[c], RL.at[c], p_xl)

        def st_k():
            out[16 * c:16 * c + 16, :] = (y_sum(xl) + RL[c]).astype(BF)

        step(nm + "m", dy_ends + ["wd"], [], mm_h)
        step(nm + "a", [nm + "rx"], [], st_a)
        step(nm + "b1", [nm + "rz1"], [], st_b1)
        step(nm + "b0", [nm + "rz0"], [], st_b0)
        ends = row_gather(
            nm, H.at[c], 2, K1_H[c], first=st_c, after=([nm + k for k in ("rf00", "rf11", "rf01", "rf10")], [])
        )
        step(nm + "f", gu_ends + ends, [], st_f)
        step(nm + "g", ["wg", "wu"], [nm + "f"], st_g)
        step(nm + "i", [nm + "c"], [], st_i)
        step(nm + "j", [nm + f"y{i}" for i in range(3)], [], st_j)
        step(nm + "k", [nm + "l"], [], st_k)

    for c in range(NC):
        chunk(c)
    run_steps(steps, wait)

    for name in msgs:
        assert name in waited
        wait_send(name)
    for cp in stores:
        cp.wait()


def grads_kernel(xt, ga, ua, dw, og, ou, od, XT, GA, UA, DW, OG, OU, isem, osem):
    T, F = GA.shape
    D = XT.shape[0]
    rows = D // 4

    def blk(ref, m):
        return ref.at[pl.ds(pl.multiple_of(m * rows, rows), rows)]

    def xt_in(m):
        return pltpu.make_async_copy(blk(xt, m), blk(XT, m), isem.at[m])

    ga_in = pltpu.make_async_copy(ga, GA, isem.at[4])
    ua_in = pltpu.make_async_copy(ua, UA, isem.at[5])
    dw_in = pltpu.make_async_copy(dw, DW, isem.at[6])
    xt_in(0).start()
    ga_in.start()
    for m in range(1, 4):
        xt_in(m).start()
    ua_in.start()
    dw_in.start()

    def out(m, first, src, dst):
        return pltpu.make_async_copy(blk(src, m), blk(dst, m), osem.at[first + m])

    ga_in.wait()

    def gate(m, _):
        xt_in(m).wait()
        x = XT[pl.ds(pl.multiple_of(m * rows, rows), rows), :]
        v = jnp.dot(x, GA[...], preferred_element_type=F32)
        OG[pl.ds(pl.multiple_of(m * rows, rows), rows), :] = v.astype(BF)
        out(m, 0, OG, og).start()
        return 0

    lax.fori_loop(0, 4, gate, 0)
    dw_in.wait()
    dw_out = pltpu.make_async_copy(DW, od, osem.at[8])
    dw_out.start()
    ua_in.wait()

    def up(m, _):
        x = XT[pl.ds(pl.multiple_of(m * rows, rows), rows), :]
        v = jnp.dot(x, UA[...], preferred_element_type=F32)
        OU[pl.ds(pl.multiple_of(m * rows, rows), rows), :] = v.astype(BF)
        out(m, 4, OU, ou).start()
        return 0

    lax.fori_loop(0, 4, up, 0)
    for m in range(4):
        out(m, 0, OG, og).wait()
        out(m, 4, OU, ou).wait()
    dw_out.wait()


def on_device(inputs, out_grad, gate_pre, up_pre, gate_weight, up_weight, down_weight):
    D, F = gate_weight.shape
    T = 1024
    any_spec = pl.BlockSpec(memory_space=pl.ANY)
    v = pltpu.VMEM
    scratch = [
        v((16, 64, D), BF), v((16, 64, D), BF),
        v((64, 16, F), BF), v((64, 16, F), BF),
        v((D, F), BF), v((D, F), BF), v((D, F), BF),
        v((NC, 16, 16, F), BF), v((NC, 8, 16, F), BF),
        v((NC, 3, 2, 16, F), BF), v((NC, 2, 16, F), BF), v((NC, 2, 2, 16, F), BF),
        v((NC, 16, 16, F), BF),
        v((NC, 16, 16, F), BF), v((NC, 16, 16, F), BF),
        v((16, 64, F // 7 if F % 7 == 0 else F), BF),
        v((D, T), BF), v((D, T), BF),
        v((NC, 8, 2, 16, D), F32), v((NC, 8, 16, D), F32),
        v((NC, 4, 2, 16, D), BF), v((NC, 3, 2, 16, D), BF),
        v((NC, 16, D), F32), v((NC, 16, D), F32),
        pltpu.SemaphoreType.DMA((N_MSG,)), pltpu.SemaphoreType.DMA((N_MSG,)), pltpu.SemaphoreType.DMA((32,)),
    ]
    sd = jax.ShapeDtypeStruct
    input_grad, ga, ua, xt, dw = pl.pallas_call(
        comm_kernel,
        out_shape=(
            sd((64, D), BF), sd((NC, 16, 16, F), BF), sd((NC, 16, 16, F), BF), sd((D, T), BF), sd((D, F), BF),
        ),
        in_specs=[any_spec] * 7,
        out_specs=(pl.BlockSpec(memory_space=pltpu.VMEM),) + (any_spec,) * 4,
        scratch_shapes=scratch,
        compiler_params=pltpu.CompilerParams(
            collective_id=0, has_side_effects=True, vmem_limit_bytes=VMEM_LIMIT
        ),
        cost_estimate=pl.CostEstimate(flops=8 * D * F * T, bytes_accessed=30 << 20, transcendentals=T * F),
        name="comm",
    )(
        inputs, out_grad, gate_pre.reshape(8, 16, F), up_pre.reshape(8, 16, F),
        gate_weight, up_weight, down_weight,
    )
    gw, uw, dw = pl.pallas_call(
        grads_kernel,
        out_shape=(sd((D, F), BF),) * 3,
        in_specs=[any_spec] * 4,
        out_specs=(any_spec,) * 3,
        scratch_shapes=[
            v((D, T), BF), v((T, F), BF), v((T, F), BF), v((D, F), BF), v((D, F), BF), v((D, F), BF),
            pltpu.SemaphoreType.DMA((7,)), pltpu.SemaphoreType.DMA((9,)),
        ],
        compiler_params=pltpu.CompilerParams(vmem_limit_bytes=VMEM_LIMIT),
        cost_estimate=pl.CostEstimate(flops=4 * D * F * T, bytes_accessed=26 << 20, transcendentals=0),
        name="weight_grads",
    )(xt, ga.reshape(T, F), ua.reshape(T, F), dw)
    return input_grad, gw, uw, dw


def solution(mesh):
    in_specs = (P("col", "row"), P("col", "row")) + (P("row", "col"),) * 5
    out_specs = (P("col", "row"), P("row", "col"), P("row", "col"), P("row", "col"))
    return jax.shard_map(
        on_device, mesh=mesh, in_specs=in_specs, out_specs=out_specs, check_vma=False
    )
```

```python
import jax
import jax.numpy as jnp
from jax import lax
from jax.experimental import pallas as pl
from jax.experimental.pallas import tpu as pltpu
from jax.sharding import PartitionSpec as P

BF = jnp.bfloat16
F32 = jnp.float32
NC = 4
N_MSG = 180
VMEM_LIMIT = 63 << 20
K1_G, K1_U, K1_H = 8, 6, (2, 2, 2, 0)

ORDER = [
    "dy0", "g0", "u0", "wd", "dy1", "g1c", "g1b", "dyfpm", "dyfym", "dyfpp", "dyfp2", "dyfy2", "dyfyp", "h0m",
    "h3m", "u1c", "h2m", "tdy", "g2b", "h1m", "g2a", "h0a", "u2a", "h0b1", "h3a", "g1a", "h0b0", "h3b0",
    "u2b", "u1b", "wgu", "h00", "h2a", "h3b1", "u1a", "u2c", "h30", "h2b1", "h1a", "h2b0", "h01c", "h1b1",
    "h01a", "h1b0", "h20", "x0", "down0", "h01b", "h02a", "h31a", "h02b", "down1", "down2", "h31b", "down3",
    "h21c", "h21a", "x1", "xfyp", "h10", "h0f", "h0e", "h0g", "h32c", "h21b", "xfym", "down4", "h22a", "xfpm",
    "h22b", "down5", "down6", "h0n", "xfy2", "xfpp", "h11c", "h11a", "h11b", "xfp2", "h0i", "h2f", "h2e",
    "h2g", "h3f", "h12a", "h12b", "h3g", "h2n", "h2i", "h3e", "h3i", "h1f", "h1g", "h3n", "h1e", "h1i", "tx",
    "h0j", "h1n", "w2", "h2j", "h3j", "w3", "w1", "h1j", "h3k", "h2k", "w0", "h0k", "h1k",
]


def run_steps(steps, wait):
    assert sorted(ORDER) == sorted(steps)
    for name in ORDER:
        msgs, _, fn = steps[name]
        for m in msgs:
            wait(m)
        fn()


def comm_kernel(
    x_in, dy_in, g_in, u_in, wg_in, wu_in, wd_in,
    out, gw_out, ua_out, xt_out, dw_out,
    X, DY, G, U, WG, WU, WD, HP, RX, SZ, RZ, RF, H, GA, UA, HT, XT, DYT, OG,
    IGP, RC, IS, RY, IX, RL,
    ssem, rsem, lsem,
):
    D = DY.shape[-1]
    F = G.shape[-1]
    row, col = lax.axis_index("row"), lax.axis_index("col")
    h, z = lax.div(row, 4), lax.rem(row, 4)
    xl, y, core = lax.div(col, 8), lax.rem(lax.div(col, 2), 4), lax.rem(col, 2)
    z1, z2, z3 = lax.rem(z + 1, 4), lax.rem(z + 2, 4), lax.rem(z + 3, 4)
    y1, y2, y3 = lax.rem(y + 1, 4), lax.rem(y + 2, 4), lax.rem(y + 3, 4)
    oh, oxl, oc = 1 - h, 1 - xl, 1 - core

    def rid(hh, zz):
        return hh * 4 + zz

    def cid(xx, yy, cc):
        return xx * 8 + yy * 2 + cc

    p_zp, p_zm, p_x = (rid(h, z1), col), (rid(h, z3), col), (rid(oh, z), col)
    p_yp, p_ym, p_y2 = (row, cid(xl, y1, core)), (row, cid(xl, y3, core)), (row, cid(xl, y2, core))
    p_xl, p_s = (row, cid(oxl, y, core)), (row, cid(xl, y, oc))

    msgs = {}
    waited = set()
    left = set()
    loads = {}
    stores = []
    steps = {}

    def send(name, src, dst, peer):
        i = len(msgs)
        msgs[name] = pltpu.make_async_remote_copy(
            src_ref=src, dst_ref=dst, send_sem=ssem.at[i], recv_sem=rsem.at[i],
            device_id=peer, device_id_type=pl.DeviceIdType.MESH,
        )
        msgs[name].start()

    def wait(name):
        if name in waited:
            return
        waited.add(name)
        if name in loads:
            loads[name].wait()
        else:
            msgs[name].wait_recv()

    def wait_send(name):
        if name not in left:
            left.add(name)
            msgs[name].wait_send()

    def copy(src, dst):
        cp = pltpu.make_async_copy(src, dst, lsem.at[len(loads) + len(stores)])
        cp.start()
        return cp

    def load(name, src, dst):
        loads[name] = copy(src, dst)

    def store(src, dst):
        stores.append(copy(src, dst))

    def step(name, waits, after, fn):
        steps[name] = (waits, after, fn)

    bar = pltpu.get_barrier_semaphore()
    peers = (p_zp, p_zm, p_x, p_yp, p_ym, p_y2, p_xl, p_s)
    for p in peers:
        pl.semaphore_signal(bar, inc=1, device_id=p, device_id_type=pl.DeviceIdType.MESH)
    pl.semaphore_wait(bar, len(peers))

    def col_gather(nm, B, src):
        own = B.at[col]

        def s0():
            for k, p in (("x", p_xl), ("yp", p_yp), ("ym", p_ym), ("y2", p_y2), ("s", p_s)):
                send(nm + k, src, own, p)
            load(nm + "own", src, own)

        def s1():
            b = B.at[cid(oxl, y, core)]
            for k, p in (("pp", p_yp), ("pm", p_ym), ("p2", p_y2), ("sx", p_s)):
                send(nm + k, b, b, p)

        def fwd(k, xx, yy):
            b = B.at[cid(xx, yy, core)]
            step(nm + "f" + k, [nm + k], [], lambda: send(nm + "s" + k, b, b, p_s))

        step(nm + "0", [], [], s0)
        step(nm + "1", [nm + "x"], [], s1)
        for k, yy in (("p", y3), ("m", y1), ("2", y2)):
            fwd("y" + k, xl, yy)
            fwd("p" + k, oxl, yy)
        return [nm + k for k in ("own", "s", "sx", "syp", "sym", "sy2", "spp", "spm", "sp2")]

    def row_gather(nm, B, n, k1, src=None, first=None, after=()):
        q, kq = n // 2, k1 // 2

        def blk(hh, zz, lo=0, cnt=n):
            return B.at[pl.ds(rid(hh, zz) * n + lo, cnt)]

        def fw(k, p, *b):
            send(nm + k, blk(*b), blk(*b), p)

        def s0():
            if first is not None:
                first()
            me = blk(h, z)
            for k, p in (("x", p_x), ("zp", p_zp), ("zm", p_zm)):
                send(nm + k, me if src is None else src, me, p)
            if src is not None:
                load(nm + "own", src, me)

        def s1a():
            fw("fa", p_zp, h, z3, 0, q)
            if k1 < n:
                fw("xa", p_x, h, z3, k1, n - k1)

        def s1b():
            fw("fb", p_zm, h, z1, q, q)
            if k1 < n:
                fw("xb", p_x, h, z1, k1, n - k1)

        def s1c():
            fw("pp", p_zp, oh, z, 0, k1)
            fw("pm", p_zm, oh, z, 0, k1)

        step(nm + "0", after[0] if after else [], after[1] if after else [], s0)
        step(nm + "1a", [nm + "zp"], [], s1a)
        step(nm + "1b", [nm + "zm"], [], s1b)
        ends = [nm + "x", nm + "fa", nm + "fb"] + ([] if src is None else [nm + "own"])
        if k1:
            step(nm + "1c", [nm + "x"], [], s1c)
            step(nm + "2a", [nm + "pp"], [], lambda: fw("pfa", p_zp, oh, z3, 0, kq))
            step(nm + "2b", [nm + "pm"], [], lambda: fw("pfb", p_zm, oh, z1, kq, kq))
            ends += [nm + "pfa", nm + "pfb"]
        if k1 < n:
            need = [nm + "fb"] + ([nm + "fa"] if k1 < q else [])
            step(nm + "2c", need, [], lambda: fw("xc", p_x, h, z2, k1, n - k1))
            ends += [nm + "xa", nm + "xb", nm + "xc"]
        return ends

    dy_ends = col_gather("dy", DY, dy_in)
    x_ends = col_gather("x", X, x_in)
    g_ends = row_gather("g", G, 8, K1_G, g_in)
    u_ends = row_gather("u", U, 8, K1_U, u_in)
    step("wd", [], [], lambda: load("wd", wd_in, WD))
    step("wgu", [], [], lambda: (load("wg", wg_in, WG), load("wu", wu_in, WU)))

    def t_x():
        def body(r, _):
            for c in range(NC):
                v = X[pl.ds(8 * r, 8), 16 * c:16 * c + 16, :].reshape(128, D)
                XT[:, pl.ds(pl.multiple_of(256 * c + r * 128, 128), 128)] = v.T
            return 0

        lax.fori_loop(0, 2, body, 0)
        store(XT, xt_out)

    def t_dy():
        def body(r, _):
            DYT[:, pl.ds(pl.multiple_of(r * 128, 128), 128)] = DY[pl.ds(2 * r, 2)].reshape(128, D).T
            return 0

        lax.fori_loop(0, 8, body, 0)

    step("tx", x_ends, [], t_x)
    step("tdy", dy_ends, [], t_dy)

    gu_ends = g_ends + u_ends
    n_down = 7 if F % 7 == 0 else 1
    fd = F // n_down

    def down_part(n):
        s = slice(fd * n, fd * (n + 1))

        def body(j, _):
            g = G[pl.ds(8 * j, 8), :, s].astype(F32)
            act = g * (0.5 * jnp.tanh(0.5 * g) + 0.5)
            v = (act * U[pl.ds(8 * j, 8), :, s].astype(F32)).astype(BF)
            HT[pl.ds(2 * j, 2)] = v.reshape(2, 64, fd)
            return 0

        lax.fori_loop(0, 8, body, 0)
        WD[:, s] = jnp.dot(DYT[...], HT[...].reshape(1024, fd), preferred_element_type=F32).astype(BF)
        if n == n_down - 1:
            store(WD, dw_out)

    for n in range(n_down):
        before = [f"down{n - 1}"] if n else ["tdy"] + [f"h{c}m" for c in range(NC)]
        step(f"down{n}", gu_ends, before, lambda n=n: down_part(n))

    def chunk(c):
        nm = f"h{c}"
        dh = D // 2

        def mm_h():
            a = DY[:, 16 * c:16 * c + 16, :].reshape(256, D)
            HP[c] = jnp.dot(a, WD[...], preferred_element_type=F32).astype(BF).reshape(16, 16, F)
            send(nm + "rx", HP.at[c, pl.ds(8 * oh, 8)], RX.at[c], p_x)

        def own_sum(zz, k):
            return HP[c, 8 * h + 2 * zz + k].astype(F32) + RX[c, 2 * zz + k].astype(F32)

        def st_a():
            SZ[c, 0, 0] = own_sum(z2, 0).astype(BF)
            send(nm + "rz0", SZ.at[c, 0, 0], RZ.at[c, 0], p_zm)
            SZ[c, 0, 1] = own_sum(z2, 1).astype(BF)
            send(nm + "rz1", SZ.at[c, 0, 1], RZ.at[c, 1], p_zp)
            SZ[c, 1, 0] = own_sum(z1, 0).astype(BF)
            send(nm + "rf00", SZ.at[c, 1, 0], RF.at[c, 0, 0], p_zp)
            SZ[c, 2, 1] = own_sum(z3, 1).astype(BF)
            send(nm + "rf11", SZ.at[c, 2, 1], RF.at[c, 1, 1], p_zm)

        def st_b1():
            SZ[c, 1, 1] = (own_sum(z1, 1) + RZ[c, 1].astype(F32)).astype(BF)
            send(nm + "rf01", SZ.at[c, 1, 1], RF.at[c, 0, 1], p_zp)

        def st_b0():
            SZ[c, 2, 0] = (own_sum(z3, 0) + RZ[c, 0].astype(F32)).astype(BF)
            send(nm + "rf10", SZ.at[c, 2, 0], RF.at[c, 1, 0], p_zm)

        def st_c():
            for k in range(2):
                H[c, 2 * row + k] = (
                    own_sum(z, k) + RF[c, 0, k].astype(F32) + RF[c, 1, k].astype(F32)
                ).astype(BF)

        def st_f():
            def body(j, _):
                g = G[4 * j + c].astype(F32)
                u = U[4 * j + c].astype(F32)
                hh = H[c, j].astype(F32)
                s = 0.5 * jnp.tanh(0.5 * g) + 0.5
                GA[c, j] = (hh * u * s * (1.0 + g * (1.0 - s))).astype(BF)
                UA[c, j] = (hh * g * s).astype(BF)
                return 0

            lax.fori_loop(0, 16, body, 0)
            store(UA.at[c], ua_out.at[c])

        def st_g(p):
            dims = (((1,), (1,)), ((), ()))
            r = slice(p * dh, (p + 1) * dh)
            v = lax.dot_general(GA[c].reshape(256, F), WG[r, :], dims, preferred_element_type=F32)
            v += lax.dot_general(UA[c].reshape(256, F), WU[r, :], dims, preferred_element_type=F32)
            IGP[c, p] = v.reshape(8, 2, 16, dh)
            send(nm + f"c{p}", IGP.at[c, p, :, oc], RC.at[c, p], p_s)

        def st_i(p):
            for xx in range(2):
                for yy in range(4):
                    m = xx * 4 + yy
                    IS[c, p, yy, xx] = (IGP[c, p, m, core] + RC[c, p, m]).astype(BF)
            for i, (yy, peer) in enumerate(((y1, p_yp), (y3, p_ym), (y2, p_y2))):
                send(nm + f"y{i}{p}", IS.at[c, p, yy], RY.at[c, p, i], peer)

        def y_sum(p, xx):
            v = IS[c, p, y, xx].astype(F32)
            for i in range(3):
                v += RY[c, p, i, xx].astype(F32)
            return v

        def st_j():
            for p in range(2):
                IX[c, p] = y_sum(p, oxl).astype(BF)
            send(nm + "l", IX.at[c], RL.at[c], p_xl)

        def st_k():
            for p in range(2):
                v = y_sum(p, xl) + RL[c, p].astype(F32)
                out[16 * c:16 * c + 16, p * dh:(p + 1) * dh] = v.astype(BF)

        step(nm + "m", dy_ends + ["wd"], [], mm_h)
        step(nm + "a", [nm + "rx"], [], st_a)
        step(nm + "b1", [nm + "rz1"], [], st_b1)
        step(nm + "b0", [nm + "rz0"], [], st_b0)
        ends = row_gather(
            nm, H.at[c], 2, K1_H[c], first=st_c, after=([nm + k for k in ("rf00", "rf11", "rf01", "rf10")], [])
        )
        step(nm + "f", gu_ends + ends, [], st_f)
        step(nm + "g", ["wg", "wu"], [nm + "f"], lambda: st_g(0))
        step(nm + "e", ["wg", "wu"], [nm + "f"], lambda: st_g(1))
        step(nm + "i", [nm + "c0"], [], lambda: st_i(0))
        step(nm + "n", [nm + "c1"], [], lambda: st_i(1))
        step(nm + "j", [nm + f"y{i}{p}" for p in range(2) for i in range(3)], [], st_j)
        step(nm + "k", [nm + "l"], [], st_k)

    for c in range(NC):
        chunk(c)

    def gate_part(n):
        r = slice(n * D // 4, (n + 1) * D // 4)
        v = jnp.dot(XT[r, :], GA[...].reshape(1024, F), preferred_element_type=F32)
        OG[r, :] = v.astype(BF)
        store(OG.at[r], gw_out.at[r])

    for n in range(4):
        step(f"w{n}", [], ["tx"] + [f"h{c}f" for c in range(NC)], lambda n=n: gate_part(n))
    run_steps(steps, wait)

    for name in msgs:
        assert name in waited
        wait_send(name)
    for cp in stores:
        cp.wait()


def grads_kernel(
    xt, ua, gw, dw, ig, ou, og, od, oi, XT, UA, GW, DW, OU, IG, sem_x, sem_u, sem_i, sem_o
):
    D = XT.shape[0]
    rows = D // 4

    def move(src, dst, sems, m):
        b = pl.ds(pl.multiple_of(m * rows, rows), rows)
        return pltpu.make_async_copy(src.at[b], dst.at[b], sems.at[m])

    ua_in = pltpu.make_async_copy(ua, UA, sem_u.at[0])
    ig_in = pltpu.make_async_copy(ig, IG, sem_u.at[1])
    ig_out = pltpu.make_async_copy(IG, oi, sem_u.at[2])
    move(xt, XT, sem_x, 0).start()
    ua_in.start()
    ig_in.start()
    for m in range(4):
        move(gw, GW, sem_i.at[0], m).start()
        move(dw, DW, sem_i.at[1], m).start()
        if m < 3:
            move(xt, XT, sem_x, m + 1).start()
    ua_in.wait()
    ig_in.wait()
    ig_out.start()

    def up(m, _):
        move(xt, XT, sem_x, m).wait()
        b = pl.ds(pl.multiple_of(m * rows, rows), rows)
        OU[b, :] = jnp.dot(XT[b, :], UA[...], preferred_element_type=F32).astype(BF)
        move(OU, ou, sem_o.at[0], m).start()
        for i, (old, buf, new) in enumerate(((gw, GW, og), (dw, DW, od))):
            move(old, buf, sem_i.at[i], m).wait()
            move(buf, new, sem_o.at[1 + i], m).start()
        return 0

    lax.fori_loop(0, 4, up, 0)
    for m in range(4):
        for i, (buf, new) in enumerate(((OU, ou), (GW, og), (DW, od))):
            move(buf, new, sem_o.at[i], m).wait()
    ig_out.wait()


def on_device(inputs, out_grad, gate_pre, up_pre, gate_weight, up_weight, down_weight):
    D, F = gate_weight.shape
    T = 1024
    any_spec = pl.BlockSpec(memory_space=pl.ANY)
    v = pltpu.VMEM
    scratch = [
        v((16, 64, D), BF), v((16, 64, D), BF),
        v((64, 16, F), BF), v((64, 16, F), BF),
        v((D, F), BF), v((D, F), BF), v((D, F), BF),
        v((NC, 16, 16, F), BF), v((NC, 8, 16, F), BF),
        v((NC, 3, 2, 16, F), BF), v((NC, 2, 16, F), BF), v((NC, 2, 2, 16, F), BF),
        v((NC, 16, 16, F), BF),
        v((NC, 16, 16, F), BF), v((NC, 16, 16, F), BF),
        v((16, 64, F // 7 if F % 7 == 0 else F), BF),
        v((D, T), BF), v((D, T), BF), v((D, F), BF),
        v((NC, 2, 8, 2, 16, D // 2), F32), v((NC, 2, 8, 16, D // 2), F32),
        v((NC, 2, 4, 2, 16, D // 2), BF), v((NC, 2, 3, 2, 16, D // 2), BF),
        v((NC, 2, 16, D // 2), BF), v((NC, 2, 16, D // 2), BF),
        pltpu.SemaphoreType.DMA((N_MSG,)), pltpu.SemaphoreType.DMA((N_MSG,)), pltpu.SemaphoreType.DMA((32,)),
    ]
    sd = jax.ShapeDtypeStruct
    input_grad, gw, ua, xt, dw = pl.pallas_call(
        comm_kernel,
        out_shape=(
            sd((64, D), BF), sd((D, F), BF), sd((NC, 16, 16, F), BF), sd((D, T), BF), sd((D, F), BF),
        ),
        in_specs=[any_spec] * 7,
        out_specs=(pl.BlockSpec(memory_space=pltpu.VMEM),) + (any_spec,) * 4,
        scratch_shapes=scratch,
        compiler_params=pltpu.CompilerParams(
            collective_id=0, has_side_effects=True, vmem_limit_bytes=VMEM_LIMIT
        ),
        cost_estimate=pl.CostEstimate(flops=10 * D * F * T, bytes_accessed=30 << 20, transcendentals=T * F),
        name="comm",
    )(
        inputs, out_grad, gate_pre.reshape(8, 16, F), up_pre.reshape(8, 16, F),
        gate_weight, up_weight, down_weight,
    )
    uw, gw, dw, input_grad = pl.pallas_call(
        grads_kernel,
        out_shape=(sd((D, F), BF),) * 3 + (sd((64, D), BF),),
        in_specs=[any_spec] * 5,
        out_specs=(any_spec,) * 4,
        scratch_shapes=[
            v((D, T), BF), v((T, F), BF), v((D, F), BF), v((D, F), BF), v((D, F), BF),
            v((64, D), BF), pltpu.SemaphoreType.DMA((4,)), pltpu.SemaphoreType.DMA((3,)),
            pltpu.SemaphoreType.DMA((2, 4)), pltpu.SemaphoreType.DMA((3, 4)),
        ],
        compiler_params=pltpu.CompilerParams(vmem_limit_bytes=VMEM_LIMIT),
        cost_estimate=pl.CostEstimate(flops=2 * D * F * T, bytes_accessed=26 << 20, transcendentals=0),
        name="weight_grads",
    )(xt, ua.reshape(T, F), gw, dw, input_grad)
    return input_grad, gw, uw, dw


def solution(mesh):
    in_specs = (P("col", "row"), P("col", "row")) + (P("row", "col"),) * 5
    out_specs = (P("col", "row"), P("row", "col"), P("row", "col"), P("row", "col"))
    return jax.shard_map(
        on_device, mesh=mesh, in_specs=in_specs, out_specs=out_specs, check_vma=False
    )
```

```python
import jax
import jax.numpy as jnp
from jax import lax
from jax.experimental import pallas as pl
from jax.experimental.pallas import tpu as pltpu
from jax.sharding import PartitionSpec as P

BF = jnp.bfloat16
F32 = jnp.float32
NC = 4
N_MSG = 180
VMEM_LIMIT = 63 << 20
K1_G, K1_U, K1_H = 6, 8, (2, 2, 2, 0)

ORDER = [
    "u0", "dy0", "g0", "dy1", "dys", "u1c", "wd", "g1b", "g1a", "dyt", "u1b", "h1m", "u2b", "u1a", "h2m",
    "u2a", "h1a", "g1c", "h3m", "h1b0", "h1b1", "h2a", "h10", "g2a", "h2b1", "g2b", "g2c", "h0m", "h2b0",
    "h11c", "tdy", "h3a", "down0", "h11a", "h11b", "h12a", "h12b", "down1", "h3b0", "x0", "h3b1", "h20",
    "h1f", "h30", "down2", "h0a", "x1", "down3", "h21a", "wgu", "h31b", "h0b1", "h0b0", "h21c", "h31a",
    "down4", "h21b", "h00", "h1g", "xs", "h32c", "h22a", "h22b", "down5", "h1i", "h01c", "h01a", "h01b",
    "h2f", "h2g", "h3f", "h02a", "h02b", "h3g", "h2i", "h0f", "h0g", "h3i", "h1j", "tx", "h0i", "h2j",
    "down6", "w0", "w3", "h3j", "w1", "h0j", "h1k", "h3k", "w2", "h2k", "h0k",
]


def run_steps(steps, wait):
    assert sorted(ORDER) == sorted(steps)
    for name in ORDER:
        msgs, _, fn = steps[name]
        for m in msgs:
            wait(m)
        fn()


def comm_kernel(
    x_in, dy_in, g_in, u_in, wg_in, wu_in, wd_in,
    out, gw_out, ua_out, xt_out, dw_out,
    X, DY, G, U, WG, WU, WD, HP, RX, SZ, RZ, RF, H, GA, UA, HT, XT, DYT, OG,
    IGP, RC, IS, RY, IX, RL,
    ssem, rsem, lsem,
):
    D = DY.shape[-1]
    F = G.shape[-1]
    row, col = lax.axis_index("row"), lax.axis_index("col")
    h, z = lax.div(row, 4), lax.rem(row, 4)
    xl, y, core = lax.div(col, 8), lax.rem(lax.div(col, 2), 4), lax.rem(col, 2)
    z1, z2, z3 = lax.rem(z + 1, 4), lax.rem(z + 2, 4), lax.rem(z + 3, 4)
    y1, y2, y3 = lax.rem(y + 1, 4), lax.rem(y + 2, 4), lax.rem(y + 3, 4)
    oh, oxl, oc = 1 - h, 1 - xl, 1 - core

    def rid(hh, zz):
        return hh * 4 + zz

    def cid(xx, yy, cc):
        return xx * 8 + yy * 2 + cc

    p_zp, p_zm, p_x = (rid(h, z1), col), (rid(h, z3), col), (rid(oh, z), col)
    p_yp, p_ym, p_y2 = (row, cid(xl, y1, core)), (row, cid(xl, y3, core)), (row, cid(xl, y2, core))
    p_xl, p_s = (row, cid(oxl, y, core)), (row, cid(xl, y, oc))

    msgs = {}
    waited = set()
    left = set()
    loads = {}
    stores = []
    steps = {}

    def send(name, src, dst, peer):
        i = len(msgs)
        msgs[name] = pltpu.make_async_remote_copy(
            src_ref=src, dst_ref=dst, send_sem=ssem.at[i], recv_sem=rsem.at[i],
            device_id=peer, device_id_type=pl.DeviceIdType.MESH,
        )
        msgs[name].start()

    def wait(name):
        if name in waited:
            return
        waited.add(name)
        if name in loads:
            loads[name].wait()
        else:
            msgs[name].wait_recv()

    def wait_send(name):
        if name not in left:
            left.add(name)
            msgs[name].wait_send()

    def copy(src, dst):
        cp = pltpu.make_async_copy(src, dst, lsem.at[len(loads) + len(stores)])
        cp.start()
        return cp

    def load(name, src, dst):
        loads[name] = copy(src, dst)

    def store(src, dst):
        stores.append(copy(src, dst))

    def step(name, waits, after, fn):
        steps[name] = (waits, after, fn)

    bar = pltpu.get_barrier_semaphore()
    peers = (p_zp, p_zm, p_x, p_yp, p_ym, p_y2, p_xl, p_s)
    for p in peers:
        pl.semaphore_signal(bar, inc=1, device_id=p, device_id_type=pl.DeviceIdType.MESH)
    pl.semaphore_wait(bar, len(peers))

    def col_gather(nm, B, src, parts):
        own = B.at[xl * 4 + y, core]
        ys = (("p", y3), ("m", y1), ("2", y2))

        def s0():
            for k, p in (("x", p_xl), ("yp", p_yp), ("ym", p_ym), ("y2", p_y2)):
                send(nm + k, src, own, p)
            load(nm + "own", src, own)

        def s1():
            b = B.at[oxl * 4 + y, core]
            for k, p in (("pp", p_yp), ("pm", p_ym), ("p2", p_y2)):
                send(nm + k, b, b, p)

        def sib(k, first, n):
            b = B.at[pl.ds(first, n), core]
            send(nm + k, b, b, p_s)

        step(nm + "0", [], [], s0)
        step(nm + "1", [nm + "x"], [], s1)
        near = [nm + "own"] + [nm + "y" + k for k, _ in ys]
        far = [nm + "x"] + [nm + "p" + k for k, _ in ys]
        if parts == 1:
            step(nm + "s", near + far, [], lambda: sib("sa", 0, 8))
            return [nm + "sa"]
        step(nm + "s", near, [], lambda: sib("sa", 4 * xl, 4))
        step(nm + "t", far, [], lambda: sib("sb", 4 * oxl, 4))
        return [nm + "sa", nm + "sb"]

    def row_gather(nm, B, n, k1, src=None, first=None, after=()):
        q, kq = n // 2, k1 // 2

        def blk(hh, zz, lo=0, cnt=n):
            return B.at[pl.ds(rid(hh, zz) * n + lo, cnt)]

        def fw(k, p, *b):
            send(nm + k, blk(*b), blk(*b), p)

        def s0():
            if first is not None:
                first()
            me = blk(h, z)
            for k, p in (("x", p_x), ("zp", p_zp), ("zm", p_zm)):
                send(nm + k, me if src is None else src, me, p)
            if src is not None:
                load(nm + "own", src, me)

        def s1a():
            fw("fa", p_zp, h, z3, 0, q)
            if k1 < n:
                fw("xa", p_x, h, z3, k1, n - k1)

        def s1b():
            fw("fb", p_zm, h, z1, q, q)
            if k1 < n:
                fw("xb", p_x, h, z1, k1, n - k1)

        def s1c():
            fw("pp", p_zp, oh, z, 0, k1)
            fw("pm", p_zm, oh, z, 0, k1)

        step(nm + "0", after[0] if after else [], after[1] if after else [], s0)
        step(nm + "1a", [nm + "zp"], [], s1a)
        step(nm + "1b", [nm + "zm"], [], s1b)
        ends = [nm + "x", nm + "fa", nm + "fb"] + ([] if src is None else [nm + "own"])
        if k1:
            step(nm + "1c", [nm + "x"], [], s1c)
            step(nm + "2a", [nm + "pp"], [], lambda: fw("pfa", p_zp, oh, z3, 0, kq))
            step(nm + "2b", [nm + "pm"], [], lambda: fw("pfb", p_zm, oh, z1, kq, kq))
            ends += [nm + "pfa", nm + "pfb"]
        if k1 < n:
            need = [nm + "fb"] + ([nm + "fa"] if k1 < q else [])
            step(nm + "2c", need, [], lambda: fw("xc", p_x, h, z2, k1, n - k1))
            ends += [nm + "xa", nm + "xb", nm + "xc"]
        return ends

    dy_ends = col_gather("dy", DY, dy_in, 2)
    x_ends = col_gather("x", X, x_in, 1)
    g_ends = row_gather("g", G, 8, K1_G, g_in)
    u_ends = row_gather("u", U, 8, K1_U, u_in)
    step("wd", [], [], lambda: load("wd", wd_in, WD))
    step("wgu", [], [], lambda: (load("wg", wg_in, WG), load("wu", wu_in, WU)))

    def t_x():
        def body(r, _):
            for c in range(NC):
                v = X[pl.ds(4 * r, 4), :, 16 * c:16 * c + 16, :].reshape(128, D)
                XT[:, pl.ds(pl.multiple_of(256 * c + r * 128, 128), 128)] = v.T
            return 0

        lax.fori_loop(0, 2, body, 0)
        store(XT, xt_out)

    def t_dy():
        def body(r, _):
            DYT[:, pl.ds(pl.multiple_of(r * 128, 128), 128)] = DY[r].reshape(128, D).T
            return 0

        lax.fori_loop(0, 8, body, 0)

    step("tx", x_ends, [], t_x)
    step("tdy", dy_ends, [], t_dy)

    gu_ends = g_ends + u_ends
    n_down = 7 if F % 7 == 0 else 1
    fd = F // n_down

    def down_part(n):
        s = slice(fd * n, fd * (n + 1))

        def body(j, _):
            g = G[pl.ds(8 * j, 8), :, s].astype(F32)
            act = g * (0.5 * jnp.tanh(0.5 * g) + 0.5)
            v = (act * U[pl.ds(8 * j, 8), :, s].astype(F32)).astype(BF)
            HT[pl.ds(2 * j, 2)] = v.reshape(2, 64, fd)
            return 0

        lax.fori_loop(0, 8, body, 0)
        WD[:, s] = jnp.dot(DYT[...], HT[...].reshape(1024, fd), preferred_element_type=F32).astype(BF)
        if n == n_down - 1:
            store(WD, dw_out)

    for n in range(n_down):
        before = [f"down{n - 1}"] if n else ["tdy"] + [f"h{c}m" for c in range(NC)]
        step(f"down{n}", gu_ends, before, lambda n=n: down_part(n))

    def chunk(c):
        nm = f"h{c}"

        def mm_h():
            a = DY[:, :, 16 * c:16 * c + 16, :].reshape(256, D)
            HP[c] = jnp.dot(a, WD[...], preferred_element_type=F32).astype(BF).reshape(16, 16, F)
            send(nm + "rx", HP.at[c, pl.ds(8 * oh, 8)], RX.at[c], p_x)

        def own_sum(zz, k):
            return HP[c, 8 * h + 2 * zz + k].astype(F32) + RX[c, 2 * zz + k].astype(F32)

        def st_a():
            SZ[c, 0, 0] = own_sum(z2, 0).astype(BF)
            send(nm + "rz0", SZ.at[c, 0, 0], RZ.at[c, 0], p_zm)
            SZ[c, 0, 1] = own_sum(z2, 1).astype(BF)
            send(nm + "rz1", SZ.at[c, 0, 1], RZ.at[c, 1], p_zp)
            SZ[c, 1, 0] = own_sum(z1, 0).astype(BF)
            send(nm + "rf00", SZ.at[c, 1, 0], RF.at[c, 0, 0], p_zp)
            SZ[c, 2, 1] = own_sum(z3, 1).astype(BF)
            send(nm + "rf11", SZ.at[c, 2, 1], RF.at[c, 1, 1], p_zm)

        def st_b1():
            SZ[c, 1, 1] = (own_sum(z1, 1) + RZ[c, 1].astype(F32)).astype(BF)
            send(nm + "rf01", SZ.at[c, 1, 1], RF.at[c, 0, 1], p_zp)

        def st_b0():
            SZ[c, 2, 0] = (own_sum(z3, 0) + RZ[c, 0].astype(F32)).astype(BF)
            send(nm + "rf10", SZ.at[c, 2, 0], RF.at[c, 1, 0], p_zm)

        def st_c():
            for k in range(2):
                H[c, 2 * row + k] = (
                    own_sum(z, k) + RF[c, 0, k].astype(F32) + RF[c, 1, k].astype(F32)
                ).astype(BF)

        def st_f():
            def body(j, _):
                g = G[4 * j + c].astype(F32)
                u = U[4 * j + c].astype(F32)
                hh = H[c, j].astype(F32)
                s = 0.5 * jnp.tanh(0.5 * g) + 0.5
                GA[c, j] = (hh * u * s * (1.0 + g * (1.0 - s))).astype(BF)
                UA[c, j] = (hh * g * s).astype(BF)
                return 0

            lax.fori_loop(0, 16, body, 0)
            store(UA.at[c], ua_out.at[c])

        def st_g():
            dims = (((1,), (1,)), ((), ()))
            v = lax.dot_general(GA[c].reshape(256, F), WG[...], dims, preferred_element_type=F32)
            v += lax.dot_general(UA[c].reshape(256, F), WU[...], dims, preferred_element_type=F32)
            IGP[c] = v.reshape(8, 2, 16, D)
            send(nm + "c", IGP.at[c, :, oc], RC.at[c], p_s)

        def st_i():
            for xx in range(2):
                for yy in range(4):
                    m = xx * 4 + yy
                    IS[c, yy, xx] = (IGP[c, m, core] + RC[c, m]).astype(BF)
            for i, (yy, p) in enumerate(((y1, p_yp), (y3, p_ym), (y2, p_y2))):
                send(nm + f"y{i}", IS.at[c, yy], RY.at[c, i], p)

        def y_sum(xx):
            v = IS[c, y, xx].astype(F32)
            for i in range(3):
                v += RY[c, i, xx].astype(F32)
            return v

        def st_j():
            IX[c] = y_sum(oxl).astype(BF)
            send(nm + "l", IX.at[c], RL.at[c], p_xl)

        def st_k():
            out[16 * c:16 * c + 16, :] = (y_sum(xl) + RL[c].astype(F32)).astype(BF)

        step(nm + "m", dy_ends + ["wd"], [], mm_h)
        step(nm + "a", [nm + "rx"], [], st_a)
        step(nm + "b1", [nm + "rz1"], [], st_b1)
        step(nm + "b0", [nm + "rz0"], [], st_b0)
        ends = row_gather(
            nm, H.at[c], 2, K1_H[c], first=st_c, after=([nm + k for k in ("rf00", "rf11", "rf01", "rf10")], [])
        )
        step(nm + "f", gu_ends + ends, [], st_f)
        step(nm + "g", ["wg", "wu"], [nm + "f"], st_g)
        step(nm + "i", [nm + "c"], [], st_i)
        step(nm + "j", [nm + f"y{i}" for i in range(3)], [], st_j)
        step(nm + "k", [nm + "l"], [], st_k)

    for c in range(NC):
        chunk(c)

    def gate_part(n):
        r = slice(n * D // 4, (n + 1) * D // 4)
        v = jnp.dot(XT[r, :], GA[...].reshape(1024, F), preferred_element_type=F32)
        OG[r, :] = v.astype(BF)
        store(OG.at[r], gw_out.at[r])

    for n in range(4):
        step(f"w{n}", [], ["tx"] + [f"h{c}f" for c in range(NC)], lambda n=n: gate_part(n))
    run_steps(steps, wait)

    for name in msgs:
        assert name in waited
        wait_send(name)
    for cp in stores:
        cp.wait()


def grads_kernel(xt, ua, gw, dw, ig, ou, og, od, oi, XT, UA, GW, DW, OU, IG, isem, osem):
    D = XT.shape[0]
    rows = D // 4

    def blk(ref, m):
        return ref.at[pl.ds(pl.multiple_of(m * rows, rows), rows)]

    def xt_in(m):
        return pltpu.make_async_copy(blk(xt, m), blk(XT, m), isem.at[m])

    def out(m):
        return pltpu.make_async_copy(blk(OU, m), blk(ou, m), osem.at[m])

    ua_in = pltpu.make_async_copy(ua, UA, isem.at[4])
    gw_in = pltpu.make_async_copy(gw, GW, isem.at[5])
    dw_in = pltpu.make_async_copy(dw, DW, isem.at[6])
    gw_out = pltpu.make_async_copy(GW, og, osem.at[4])
    dw_out = pltpu.make_async_copy(DW, od, osem.at[5])
    ig_in = pltpu.make_async_copy(ig, IG, isem.at[7])
    ig_out = pltpu.make_async_copy(IG, oi, osem.at[6])
    xt_in(0).start()
    ua_in.start()
    gw_in.start()
    for m in range(1, 4):
        xt_in(m).start()
    dw_in.start()
    ig_in.start()
    ua_in.wait()

    def up(m, _):
        xt_in(m).wait()
        x = XT[pl.ds(pl.multiple_of(m * rows, rows), rows), :]
        v = jnp.dot(x, UA[...], preferred_element_type=F32)
        OU[pl.ds(pl.multiple_of(m * rows, rows), rows), :] = v.astype(BF)
        out(m).start()
        return 0

    lax.fori_loop(0, 1, up, 0)
    gw_in.wait()
    gw_out.start()
    lax.fori_loop(1, 2, up, 0)
    dw_in.wait()
    dw_out.start()
    ig_in.wait()
    ig_out.start()
    lax.fori_loop(2, 4, up, 0)
    for m in range(4):
        out(m).wait()
    gw_out.wait()
    dw_out.wait()
    ig_out.wait()


def on_device(inputs, out_grad, gate_pre, up_pre, gate_weight, up_weight, down_weight):
    D, F = gate_weight.shape
    T = 1024
    any_spec = pl.BlockSpec(memory_space=pl.ANY)
    v = pltpu.VMEM
    scratch = [
        v((8, 2, 64, D), BF), v((8, 2, 64, D), BF),
        v((64, 16, F), BF), v((64, 16, F), BF),
        v((D, F), BF), v((D, F), BF), v((D, F), BF),
        v((NC, 16, 16, F), BF), v((NC, 8, 16, F), BF),
        v((NC, 3, 2, 16, F), BF), v((NC, 2, 16, F), BF), v((NC, 2, 2, 16, F), BF),
        v((NC, 16, 16, F), BF),
        v((NC, 16, 16, F), BF), v((NC, 16, 16, F), BF),
        v((16, 64, F // 7 if F % 7 == 0 else F), BF),
        v((D, T), BF), v((D, T), BF), v((D, F), BF),
        v((NC, 8, 2, 16, D), F32), v((NC, 8, 16, D), F32),
        v((NC, 4, 2, 16, D), BF), v((NC, 3, 2, 16, D), BF),
        v((NC, 16, D), BF), v((NC, 16, D), BF),
        pltpu.SemaphoreType.DMA((N_MSG,)), pltpu.SemaphoreType.DMA((N_MSG,)), pltpu.SemaphoreType.DMA((32,)),
    ]
    sd = jax.ShapeDtypeStruct
    input_grad, gw, ua, xt, dw = pl.pallas_call(
        comm_kernel,
        out_shape=(
            sd((64, D), BF), sd((D, F), BF), sd((NC, 16, 16, F), BF), sd((D, T), BF), sd((D, F), BF),
        ),
        in_specs=[any_spec] * 7,
        out_specs=(pl.BlockSpec(memory_space=pltpu.VMEM),) + (any_spec,) * 4,
        scratch_shapes=scratch,
        compiler_params=pltpu.CompilerParams(
            collective_id=0, has_side_effects=True, vmem_limit_bytes=VMEM_LIMIT
        ),
        cost_estimate=pl.CostEstimate(flops=10 * D * F * T, bytes_accessed=30 << 20, transcendentals=T * F),
        name="comm",
    )(
        inputs, out_grad, gate_pre.reshape(8, 16, F), up_pre.reshape(8, 16, F),
        gate_weight, up_weight, down_weight,
    )
    uw, gw, dw, input_grad = pl.pallas_call(
        grads_kernel,
        out_shape=(sd((D, F), BF),) * 3 + (sd((64, D), BF),),
        in_specs=[any_spec] * 5,
        out_specs=(any_spec,) * 4,
        scratch_shapes=[
            v((D, T), BF), v((T, F), BF), v((D, F), BF), v((D, F), BF), v((D, F), BF),
            v((64, D), BF), pltpu.SemaphoreType.DMA((8,)), pltpu.SemaphoreType.DMA((7,)),
        ],
        compiler_params=pltpu.CompilerParams(vmem_limit_bytes=VMEM_LIMIT),
        cost_estimate=pl.CostEstimate(flops=2 * D * F * T, bytes_accessed=26 << 20, transcendentals=0),
        name="weight_grads",
    )(xt, ua.reshape(T, F), gw, dw, input_grad)
    return input_grad, gw, uw, dw


def solution(mesh):
    in_specs = (P("col", "row"), P("col", "row")) + (P("row", "col"),) * 5
    out_specs = (P("col", "row"), P("row", "col"), P("row", "col"), P("row", "col"))
    return jax.shard_map(
        on_device, mesh=mesh, in_specs=in_specs, out_specs=out_specs, check_vma=False
    )
```

```python
import jax
import jax.numpy as jnp
from jax import lax
from jax.experimental import pallas as pl
from jax.experimental.pallas import tpu as pltpu
from jax.sharding import PartitionSpec as P

BF = jnp.bfloat16
F32 = jnp.float32
NC = 4
N_MSG = 180
LAG = 30
VMEM_LIMIT = 63 << 20
K1_G, K1_U, K1_H = 6, 8, (2, 2, 2, 0)

ORDER = [
    "u0", "dy0", "g0", "dy1", "dys", "u1c", "wd", "g1b", "g1a", "dyt", "u1b", "h1m", "u2b", "u1a", "h2m",
    "u2a", "h1a", "g1c", "h3m", "h1b0", "h1b1", "h2a", "h10", "g2a", "h2b1", "g2b", "g2c", "h0m", "h2b0",
    "h11c", "tdy", "h3a", "down0", "h11a", "h11b", "h12a", "h12b", "down1", "h3b0", "x0", "h3b1", "h20",
    "h1f", "h30", "down2", "h0a", "x1", "down3", "h21a", "wgu", "h31b", "h0b1", "h0b0", "h21c", "h31a",
    "down4", "h21b", "h00", "h1g", "xs", "h32c", "h22a", "h22b", "down5", "h1i", "h01c", "h01a", "h01b",
    "h2f", "h2g", "h3f", "h02a", "h02b", "h3g", "h2i", "h0f", "h0g", "h3i", "h1j", "tx", "h0i", "h2j",
    "down6", "w0", "w3", "h3j", "w1", "h0j", "h1k", "h3k", "w2", "h2k", "h0k",
]


def run_steps(steps, wait, sent, wait_send):
    assert sorted(ORDER) == sorted(steps)
    ends = []
    for name in ORDER:
        msgs, _, fn = steps[name]
        for m in msgs:
            wait(m)
        fn()
        ends.append(len(sent))
        if len(ends) > LAG:
            first = ends[-LAG - 2] if len(ends) > LAG + 1 else 0
            for m in list(sent)[first:ends[-LAG - 1]]:
                wait_send(m)


def comm_kernel(
    x_in, dy_in, g_in, u_in, wg_in, wu_in, wd_in,
    out, gw_out, ua_out, xt_out, dw_out,
    X, DY, G, U, WG, WU, WD, HP, RX, SZ, RZ, RF, H, GA, UA, HT, XT, DYT, OG,
    IGP, RC, IS, RY, IX, RL,
    ssem, rsem, lsem,
):
    D = DY.shape[-1]
    F = G.shape[-1]
    row, col = lax.axis_index("row"), lax.axis_index("col")
    h, z = lax.div(row, 4), lax.rem(row, 4)
    xl, y, core = lax.div(col, 8), lax.rem(lax.div(col, 2), 4), lax.rem(col, 2)
    z1, z2, z3 = lax.rem(z + 1, 4), lax.rem(z + 2, 4), lax.rem(z + 3, 4)
    y1, y2, y3 = lax.rem(y + 1, 4), lax.rem(y + 2, 4), lax.rem(y + 3, 4)
    oh, oxl, oc = 1 - h, 1 - xl, 1 - core

    def rid(hh, zz):
        return hh * 4 + zz

    def cid(xx, yy, cc):
        return xx * 8 + yy * 2 + cc

    p_zp, p_zm, p_x = (rid(h, z1), col), (rid(h, z3), col), (rid(oh, z), col)
    p_yp, p_ym, p_y2 = (row, cid(xl, y1, core)), (row, cid(xl, y3, core)), (row, cid(xl, y2, core))
    p_xl, p_s = (row, cid(oxl, y, core)), (row, cid(xl, y, oc))

    msgs = {}
    waited = set()
    left = set()
    loads = {}
    stores = []
    steps = {}

    def send(name, src, dst, peer):
        i = len(msgs)
        msgs[name] = pltpu.make_async_remote_copy(
            src_ref=src, dst_ref=dst, send_sem=ssem.at[i], recv_sem=rsem.at[i],
            device_id=peer, device_id_type=pl.DeviceIdType.MESH,
        )
        msgs[name].start()

    def wait(name):
        if name in waited:
            return
        waited.add(name)
        if name in loads:
            loads[name].wait()
        else:
            msgs[name].wait_recv()

    def wait_send(name):
        if name not in left:
            left.add(name)
            msgs[name].wait_send()

    def copy(src, dst):
        cp = pltpu.make_async_copy(src, dst, lsem.at[len(loads) + len(stores)])
        cp.start()
        return cp

    def load(name, src, dst):
        loads[name] = copy(src, dst)

    def store(src, dst):
        stores.append(copy(src, dst))

    def step(name, waits, after, fn):
        steps[name] = (waits, after, fn)

    bar = pltpu.get_barrier_semaphore()
    peers = (p_zp, p_zm, p_x, p_yp, p_ym, p_y2, p_xl, p_s)
    for p in peers:
        pl.semaphore_signal(bar, inc=1, device_id=p, device_id_type=pl.DeviceIdType.MESH)
    pl.semaphore_wait(bar, len(peers))

    def col_gather(nm, B, src, parts):
        own = B.at[xl * 4 + y, core]
        ys = (("p", y3), ("m", y1), ("2", y2))

        def s0():
            for k, p in (("x", p_xl), ("yp", p_yp), ("ym", p_ym), ("y2", p_y2)):
                send(nm + k, src, own, p)
            load(nm + "own", src, own)

        def s1():
            b = B.at[oxl * 4 + y, core]
            for k, p in (("pp", p_yp), ("pm", p_ym), ("p2", p_y2)):
                send(nm + k, b, b, p)

        def sib(k, first, n):
            b = B.at[pl.ds(first, n), core]
            send(nm + k, b, b, p_s)

        step(nm + "0", [], [], s0)
        step(nm + "1", [nm + "x"], [], s1)
        near = [nm + "own"] + [nm + "y" + k for k, _ in ys]
        far = [nm + "x"] + [nm + "p" + k for k, _ in ys]
        if parts == 1:
            step(nm + "s", near + far, [], lambda: sib("sa", 0, 8))
            return [nm + "sa"]
        step(nm + "s", near, [], lambda: sib("sa", 4 * xl, 4))
        step(nm + "t", far, [], lambda: sib("sb", 4 * oxl, 4))
        return [nm + "sa", nm + "sb"]

    def row_gather(nm, B, n, k1, src=None, first=None, after=()):
        q, kq = n // 2, k1 // 2

        def blk(hh, zz, lo=0, cnt=n):
            return B.at[pl.ds(rid(hh, zz) * n + lo, cnt)]

        def fw(k, p, *b):
            send(nm + k, blk(*b), blk(*b), p)

        def s0():
            if first is not None:
                first()
            me = blk(h, z)
            for k, p in (("x", p_x), ("zp", p_zp), ("zm", p_zm)):
                send(nm + k, me if src is None else src, me, p)
            if src is not None:
                load(nm + "own", src, me)

        def s1a():
            fw("fa", p_zp, h, z3, 0, q)
            if k1 < n:
                fw("xa", p_x, h, z3, k1, n - k1)

        def s1b():
            fw("fb", p_zm, h, z1, q, q)
            if k1 < n:
                fw("xb", p_x, h, z1, k1, n - k1)

        def s1c():
            fw("pp", p_zp, oh, z, 0, k1)
            fw("pm", p_zm, oh, z, 0, k1)

        step(nm + "0", after[0] if after else [], after[1] if after else [], s0)
        step(nm + "1a", [nm + "zp"], [], s1a)
        step(nm + "1b", [nm + "zm"], [], s1b)
        ends = [nm + "x", nm + "fa", nm + "fb"] + ([] if src is None else [nm + "own"])
        if k1:
            step(nm + "1c", [nm + "x"], [], s1c)
            step(nm + "2a", [nm + "pp"], [], lambda: fw("pfa", p_zp, oh, z3, 0, kq))
            step(nm + "2b", [nm + "pm"], [], lambda: fw("pfb", p_zm, oh, z1, kq, kq))
            ends += [nm + "pfa", nm + "pfb"]
        if k1 < n:
            need = [nm + "fb"] + ([nm + "fa"] if k1 < q else [])
            step(nm + "2c", need, [], lambda: fw("xc", p_x, h, z2, k1, n - k1))
            ends += [nm + "xa", nm + "xb", nm + "xc"]
        return ends

    dy_ends = col_gather("dy", DY, dy_in, 2)
    x_ends = col_gather("x", X, x_in, 1)
    g_ends = row_gather("g", G, 8, K1_G, g_in)
    u_ends = row_gather("u", U, 8, K1_U, u_in)
    step("wd", [], [], lambda: load("wd", wd_in, WD))
    step("wgu", [], [], lambda: (load("wg", wg_in, WG), load("wu", wu_in, WU)))

    def t_x():
        def body(r, _):
            for c in range(NC):
                v = X[pl.ds(4 * r, 4), :, 16 * c:16 * c + 16, :].reshape(128, D)
                XT[:, pl.ds(pl.multiple_of(256 * c + r * 128, 128), 128)] = v.T
            return 0

        lax.fori_loop(0, 2, body, 0)
        store(XT, xt_out)

    def t_dy():
        def body(r, _):
            DYT[:, pl.ds(pl.multiple_of(r * 128, 128), 128)] = DY[r].reshape(128, D).T
            return 0

        lax.fori_loop(0, 8, body, 0)

    step("tx", x_ends, [], t_x)
    step("tdy", dy_ends, [], t_dy)

    gu_ends = g_ends + u_ends
    n_down = 7 if F % 7 == 0 else 1
    fd = F // n_down

    def down_part(n):
        s = slice(fd * n, fd * (n + 1))

        def body(j, _):
            g = G[pl.ds(8 * j, 8), :, s].astype(F32)
            act = g * (0.5 * jnp.tanh(0.5 * g) + 0.5)
            v = (act * U[pl.ds(8 * j, 8), :, s].astype(F32)).astype(BF)
            HT[pl.ds(2 * j, 2)] = v.reshape(2, 64, fd)
            return 0

        lax.fori_loop(0, 8, body, 0)
        WD[:, s] = jnp.dot(DYT[...], HT[...].reshape(1024, fd), preferred_element_type=F32).astype(BF)
        if n == n_down - 1:
            store(WD, dw_out)

    for n in range(n_down):
        before = [f"down{n - 1}"] if n else ["tdy"] + [f"h{c}m" for c in range(NC)]
        step(f"down{n}", gu_ends, before, lambda n=n: down_part(n))

    def chunk(c):
        nm = f"h{c}"

        def mm_h():
            a = DY[:, :, 16 * c:16 * c + 16, :].reshape(256, D)
            HP[c] = jnp.dot(a, WD[...], preferred_element_type=F32).astype(BF).reshape(16, 16, F)
            send(nm + "rx", HP.at[c, pl.ds(8 * oh, 8)], RX.at[c], p_x)

        def own_sum(zz, k):
            return HP[c, 8 * h + 2 * zz + k].astype(F32) + RX[c, 2 * zz + k].astype(F32)

        def st_a():
            SZ[c, 0, 0] = own_sum(z2, 0).astype(BF)
            send(nm + "rz0", SZ.at[c, 0, 0], RZ.at[c, 0], p_zm)
            SZ[c, 0, 1] = own_sum(z2, 1).astype(BF)
            send(nm + "rz1", SZ.at[c, 0, 1], RZ.at[c, 1], p_zp)
            SZ[c, 1, 0] = own_sum(z1, 0).astype(BF)
            send(nm + "rf00", SZ.at[c, 1, 0], RF.at[c, 0, 0], p_zp)
            SZ[c, 2, 1] = own_sum(z3, 1).astype(BF)
            send(nm + "rf11", SZ.at[c, 2, 1], RF.at[c, 1, 1], p_zm)

        def st_b1():
            SZ[c, 1, 1] = (own_sum(z1, 1) + RZ[c, 1].astype(F32)).astype(BF)
            send(nm + "rf01", SZ.at[c, 1, 1], RF.at[c, 0, 1], p_zp)

        def st_b0():
            SZ[c, 2, 0] = (own_sum(z3, 0) + RZ[c, 0].astype(F32)).astype(BF)
            send(nm + "rf10", SZ.at[c, 2, 0], RF.at[c, 1, 0], p_zm)

        def st_c():
            for k in range(2):
                H[c, 2 * row + k] = (
                    own_sum(z, k) + RF[c, 0, k].astype(F32) + RF[c, 1, k].astype(F32)
                ).astype(BF)

        def st_f():
            def body(j, _):
                g = G[4 * j + c].astype(F32)
                u = U[4 * j + c].astype(F32)
                hh = H[c, j].astype(F32)
                s = 0.5 * jnp.tanh(0.5 * g) + 0.5
                GA[c, j] = (hh * u * s * (1.0 + g * (1.0 - s))).astype(BF)
                UA[c, j] = (hh * g * s).astype(BF)
                return 0

            lax.fori_loop(0, 16, body, 0)
            store(UA.at[c], ua_out.at[c])

        def st_g():
            dims = (((1,), (1,)), ((), ()))
            v = lax.dot_general(GA[c].reshape(256, F), WG[...], dims, preferred_element_type=F32)
            v += lax.dot_general(UA[c].reshape(256, F), WU[...], dims, preferred_element_type=F32)
            IGP[c] = v.reshape(8, 2, 16, D)
            send(nm + "c", IGP.at[c, :, oc], RC.at[c], p_s)

        def st_i():
            for xx in range(2):
                for yy in range(4):
                    m = xx * 4 + yy
                    IS[c, yy, xx] = (IGP[c, m, core] + RC[c, m]).astype(BF)
            for i, (yy, p) in enumerate(((y1, p_yp), (y3, p_ym), (y2, p_y2))):
                send(nm + f"y{i}", IS.at[c, yy], RY.at[c, i], p)

        def y_sum(xx):
            v = IS[c, y, xx].astype(F32)
            for i in range(3):
                v += RY[c, i, xx].astype(F32)
            return v

        def st_j():
            IX[c] = y_sum(oxl).astype(BF)
            send(nm + "l", IX.at[c], RL.at[c], p_xl)

        def st_k():
            out[16 * c:16 * c + 16, :] = (y_sum(xl) + RL[c].astype(F32)).astype(BF)

        step(nm + "m", dy_ends + ["wd"], [], mm_h)
        step(nm + "a", [nm + "rx"], [], st_a)
        step(nm + "b1", [nm + "rz1"], [], st_b1)
        step(nm + "b0", [nm + "rz0"], [], st_b0)
        ends = row_gather(
            nm, H.at[c], 2, K1_H[c], first=st_c, after=([nm + k for k in ("rf00", "rf11", "rf01", "rf10")], [])
        )
        step(nm + "f", gu_ends + ends, [], st_f)
        step(nm + "g", ["wg", "wu"], [nm + "f"], st_g)
        step(nm + "i", [nm + "c"], [], st_i)
        step(nm + "j", [nm + f"y{i}" for i in range(3)], [], st_j)
        step(nm + "k", [nm + "l"], [], st_k)

    for c in range(NC):
        chunk(c)

    def gate_part(n):
        r = slice(n * D // 4, (n + 1) * D // 4)
        v = jnp.dot(XT[r, :], GA[...].reshape(1024, F), preferred_element_type=F32)
        OG[r, :] = v.astype(BF)
        store(OG.at[r], gw_out.at[r])

    for n in range(4):
        step(f"w{n}", [], ["tx"] + [f"h{c}f" for c in range(NC)], lambda n=n: gate_part(n))
    run_steps(steps, wait, msgs, wait_send)

    for name in msgs:
        assert name in waited
        wait_send(name)
    for cp in stores:
        cp.wait()


def grads_kernel(xt, ua, gw, dw, ig, ou, og, od, oi, XT, UA, GW, DW, OU, IG, isem, osem):
    D = XT.shape[0]
    rows = D // 4

    def blk(ref, m):
        return ref.at[pl.ds(pl.multiple_of(m * rows, rows), rows)]

    def xt_in(m):
        return pltpu.make_async_copy(blk(xt, m), blk(XT, m), isem.at[m])

    def out(m):
        return pltpu.make_async_copy(blk(OU, m), blk(ou, m), osem.at[m])

    ua_in = pltpu.make_async_copy(ua, UA, isem.at[4])
    gw_in = pltpu.make_async_copy(gw, GW, isem.at[5])
    dw_in = pltpu.make_async_copy(dw, DW, isem.at[6])
    gw_out = pltpu.make_async_copy(GW, og, osem.at[4])
    dw_out = pltpu.make_async_copy(DW, od, osem.at[5])
    ig_in = pltpu.make_async_copy(ig, IG, isem.at[7])
    ig_out = pltpu.make_async_copy(IG, oi, osem.at[6])
    xt_in(0).start()
    ua_in.start()
    gw_in.start()
    for m in range(1, 4):
        xt_in(m).start()
    dw_in.start()
    ig_in.start()
    ua_in.wait()

    def up(m, _):
        xt_in(m).wait()
        x = XT[pl.ds(pl.multiple_of(m * rows, rows), rows), :]
        v = jnp.dot(x, UA[...], preferred_element_type=F32)
        OU[pl.ds(pl.multiple_of(m * rows, rows), rows), :] = v.astype(BF)
        out(m).start()
        return 0

    lax.fori_loop(0, 1, up, 0)
    gw_in.wait()
    gw_out.start()
    lax.fori_loop(1, 2, up, 0)
    dw_in.wait()
    dw_out.start()
    ig_in.wait()
    ig_out.start()
    lax.fori_loop(2, 4, up, 0)
    for m in range(4):
        out(m).wait()
    gw_out.wait()
    dw_out.wait()
    ig_out.wait()


def on_device(inputs, out_grad, gate_pre, up_pre, gate_weight, up_weight, down_weight):
    D, F = gate_weight.shape
    T = 1024
    any_spec = pl.BlockSpec(memory_space=pl.ANY)
    v = pltpu.VMEM
    scratch = [
        v((8, 2, 64, D), BF), v((8, 2, 64, D), BF),
        v((64, 16, F), BF), v((64, 16, F), BF),
        v((D, F), BF), v((D, F), BF), v((D, F), BF),
        v((NC, 16, 16, F), BF), v((NC, 8, 16, F), BF),
        v((NC, 3, 2, 16, F), BF), v((NC, 2, 16, F), BF), v((NC, 2, 2, 16, F), BF),
        v((NC, 16, 16, F), BF),
        v((NC, 16, 16, F), BF), v((NC, 16, 16, F), BF),
        v((16, 64, F // 7 if F % 7 == 0 else F), BF),
        v((D, T), BF), v((D, T), BF), v((D, F), BF),
        v((NC, 8, 2, 16, D), F32), v((NC, 8, 16, D), F32),
        v((NC, 4, 2, 16, D), BF), v((NC, 3, 2, 16, D), BF),
        v((NC, 16, D), BF), v((NC, 16, D), BF),
        pltpu.SemaphoreType.DMA((N_MSG,)), pltpu.SemaphoreType.DMA((N_MSG,)), pltpu.SemaphoreType.DMA((32,)),
    ]
    sd = jax.ShapeDtypeStruct
    input_grad, gw, ua, xt, dw = pl.pallas_call(
        comm_kernel,
        out_shape=(
            sd((64, D), BF), sd((D, F), BF), sd((NC, 16, 16, F), BF), sd((D, T), BF), sd((D, F), BF),
        ),
        in_specs=[any_spec] * 7,
        out_specs=(pl.BlockSpec(memory_space=pltpu.VMEM),) + (any_spec,) * 4,
        scratch_shapes=scratch,
        compiler_params=pltpu.CompilerParams(
            collective_id=0, has_side_effects=True, vmem_limit_bytes=VMEM_LIMIT
        ),
        cost_estimate=pl.CostEstimate(flops=10 * D * F * T, bytes_accessed=30 << 20, transcendentals=T * F),
        name="comm",
    )(
        inputs, out_grad, gate_pre.reshape(8, 16, F), up_pre.reshape(8, 16, F),
        gate_weight, up_weight, down_weight,
    )
    uw, gw, dw, input_grad = pl.pallas_call(
        grads_kernel,
        out_shape=(sd((D, F), BF),) * 3 + (sd((64, D), BF),),
        in_specs=[any_spec] * 5,
        out_specs=(any_spec,) * 4,
        scratch_shapes=[
            v((D, T), BF), v((T, F), BF), v((D, F), BF), v((D, F), BF), v((D, F), BF),
            v((64, D), BF), pltpu.SemaphoreType.DMA((8,)), pltpu.SemaphoreType.DMA((7,)),
        ],
        compiler_params=pltpu.CompilerParams(vmem_limit_bytes=VMEM_LIMIT),
        cost_estimate=pl.CostEstimate(flops=2 * D * F * T, bytes_accessed=26 << 20, transcendentals=0),
        name="weight_grads",
    )(xt, ua.reshape(T, F), gw, dw, input_grad)
    return input_grad, gw, uw, dw


def solution(mesh):
    in_specs = (P("col", "row"), P("col", "row")) + (P("row", "col"),) * 5
    out_specs = (P("col", "row"), P("row", "col"), P("row", "col"), P("row", "col"))
    return jax.shard_map(
        on_device, mesh=mesh, in_specs=in_specs, out_specs=out_specs, check_vma=False
    )
```

```python
import jax
import jax.numpy as jnp
from jax import lax
from jax.experimental import pallas as pl
from jax.experimental.pallas import tpu as pltpu
from jax.sharding import PartitionSpec as P

BF = jnp.bfloat16
F32 = jnp.float32
NC = 4
N_MSG = 180
VMEM_LIMIT = 63 << 20
K1_G, K1_U, K1_H = 6, 8, (2, 2, 2, 0)

ORDER = [
    "dy0", "u0", "wgu", "dy1", "g0", "dys", "wd", "dyt", "h0m", "u1c", "g1c", "h3m", "h1m", "u1a", "h2m",
    "h0a", "u2a", "u2b", "h0b0", "h0b1", "u1b", "g1a", "h3a", "g1b", "g2b", "h3b0", "h1a", "h3b1", "h00",
    "g2a", "h1b0", "h1b1", "h2a", "tdy", "g2c", "h30", "h10", "h2b0", "h2b1", "h01c", "h31b", "h31a", "down0",
    "down1", "h01a", "h01b", "down2", "h02a", "h02b", "h11c", "h20", "down3", "h11a", "h32c", "x0", "h0f",
    "h0g", "h11b", "h12a", "h12b", "h21c", "h21a", "h21b", "h0i", "h3f", "x1", "h3g", "h1f", "h22a", "h22b",
    "h1g", "h3i", "h2f", "h2g", "h1i", "down4", "h2i", "h3j", "xs", "down5", "down6", "h0j", "h1j", "tx",
    "w1", "h2j", "h0k", "h3k", "h1k", "w0", "h2k",
]


def run_steps(steps, wait):
    assert sorted(ORDER) == sorted(steps)
    for name in ORDER:
        msgs, _, fn = steps[name]
        for m in msgs:
            wait(m)
        fn()


def comm_kernel(
    x_in, dy_in, g_in, u_in, wg_in, wu_in, wd_in,
    out, gw_out, ga_out, ua_out, xt_out, dw_out,
    X, DY, G, U, WG, WU, WD, HP, RX, SZ, RZ, RF, H, GA, UA, HT, XT, DYT, OG,
    IGP, RC, IS, RY, IX, RL,
    ssem, rsem, lsem,
):
    D = DY.shape[-1]
    F = G.shape[-1]
    row, col = lax.axis_index("row"), lax.axis_index("col")
    h, z = lax.div(row, 4), lax.rem(row, 4)
    xl, y, core = lax.div(col, 8), lax.rem(lax.div(col, 2), 4), lax.rem(col, 2)
    z1, z2, z3 = lax.rem(z + 1, 4), lax.rem(z + 2, 4), lax.rem(z + 3, 4)
    y1, y2, y3 = lax.rem(y + 1, 4), lax.rem(y + 2, 4), lax.rem(y + 3, 4)
    oh, oxl, oc = 1 - h, 1 - xl, 1 - core

    def rid(hh, zz):
        return hh * 4 + zz

    def cid(xx, yy, cc):
        return xx * 8 + yy * 2 + cc

    p_zp, p_zm, p_x = (rid(h, z1), col), (rid(h, z3), col), (rid(oh, z), col)
    p_yp, p_ym, p_y2 = (row, cid(xl, y1, core)), (row, cid(xl, y3, core)), (row, cid(xl, y2, core))
    p_xl, p_s = (row, cid(oxl, y, core)), (row, cid(xl, y, oc))

    msgs = {}
    waited = set()
    left = set()
    loads = {}
    stores = []
    steps = {}

    def send(name, src, dst, peer):
        i = len(msgs)
        msgs[name] = pltpu.make_async_remote_copy(
            src_ref=src, dst_ref=dst, send_sem=ssem.at[i], recv_sem=rsem.at[i],
            device_id=peer, device_id_type=pl.DeviceIdType.MESH,
        )
        msgs[name].start()

    def wait(name):
        if name in waited:
            return
        waited.add(name)
        if name in loads:
            loads[name].wait()
        else:
            msgs[name].wait_recv()

    def wait_send(name):
        if name not in left:
            left.add(name)
            msgs[name].wait_send()

    def copy(src, dst):
        cp = pltpu.make_async_copy(src, dst, lsem.at[len(loads) + len(stores)])
        cp.start()
        return cp

    def load(name, src, dst):
        loads[name] = copy(src, dst)

    def store(src, dst):
        stores.append(copy(src, dst))

    def step(name, waits, after, fn):
        steps[name] = (waits, after, fn)

    bar = pltpu.get_barrier_semaphore()
    peers = (p_zp, p_zm, p_x, p_yp, p_ym, p_y2, p_xl, p_s)
    for p in peers:
        pl.semaphore_signal(bar, inc=1, device_id=p, device_id_type=pl.DeviceIdType.MESH)
    pl.semaphore_wait(bar, len(peers))

    def col_gather(nm, B, src, parts):
        own = B.at[xl * 4 + y, core]
        ys = (("p", y3), ("m", y1), ("2", y2))

        def s0():
            for k, p in (("x", p_xl), ("yp", p_yp), ("ym", p_ym), ("y2", p_y2)):
                send(nm + k, src, own, p)
            load(nm + "own", src, own)

        def s1():
            b = B.at[oxl * 4 + y, core]
            for k, p in (("pp", p_yp), ("pm", p_ym), ("p2", p_y2)):
                send(nm + k, b, b, p)

        def sib(k, first, n):
            b = B.at[pl.ds(first, n), core]
            send(nm + k, b, b, p_s)

        step(nm + "0", [], [], s0)
        step(nm + "1", [nm + "x"], [], s1)
        near = [nm + "own"] + [nm + "y" + k for k, _ in ys]
        far = [nm + "x"] + [nm + "p" + k for k, _ in ys]
        if parts == 1:
            step(nm + "s", near + far, [], lambda: sib("sa", 0, 8))
            return [nm + "sa"]
        step(nm + "s", near, [], lambda: sib("sa", 4 * xl, 4))
        step(nm + "t", far, [], lambda: sib("sb", 4 * oxl, 4))
        return [nm + "sa", nm + "sb"]

    def row_gather(nm, B, n, k1, src=None, first=None, after=()):
        q, kq = n // 2, k1 // 2

        def blk(hh, zz, lo=0, cnt=n):
            return B.at[pl.ds(rid(hh, zz) * n + lo, cnt)]

        def fw(k, p, *b):
            send(nm + k, blk(*b), blk(*b), p)

        def s0():
            if first is not None:
                first()
            me = blk(h, z)
            for k, p in (("x", p_x), ("zp", p_zp), ("zm", p_zm)):
                send(nm + k, me if src is None else src, me, p)
            if src is not None:
                load(nm + "own", src, me)

        def s1a():
            fw("fa", p_zp, h, z3, 0, q)
            if k1 < n:
                fw("xa", p_x, h, z3, k1, n - k1)

        def s1b():
            fw("fb", p_zm, h, z1, q, q)
            if k1 < n:
                fw("xb", p_x, h, z1, k1, n - k1)

        def s1c():
            fw("pp", p_zp, oh, z, 0, k1)
            fw("pm", p_zm, oh, z, 0, k1)

        step(nm + "0", after[0] if after else [], after[1] if after else [], s0)
        step(nm + "1a", [nm + "zp"], [], s1a)
        step(nm + "1b", [nm + "zm"], [], s1b)
        ends = [nm + "x", nm + "fa", nm + "fb"] + ([] if src is None else [nm + "own"])
        if k1:
            step(nm + "1c", [nm + "x"], [], s1c)
            step(nm + "2a", [nm + "pp"], [], lambda: fw("pfa", p_zp, oh, z3, 0, kq))
            step(nm + "2b", [nm + "pm"], [], lambda: fw("pfb", p_zm, oh, z1, kq, kq))
            ends += [nm + "pfa", nm + "pfb"]
        if k1 < n:
            need = [nm + "fb"] + ([nm + "fa"] if k1 < q else [])
            step(nm + "2c", need, [], lambda: fw("xc", p_x, h, z2, k1, n - k1))
            ends += [nm + "xa", nm + "xb", nm + "xc"]
        return ends

    dy_ends = col_gather("dy", DY, dy_in, 2)
    x_ends = col_gather("x", X, x_in, 1)
    g_ends = row_gather("g", G, 8, K1_G, g_in)
    u_ends = row_gather("u", U, 8, K1_U, u_in)
    step("wd", [], [], lambda: load("wd", wd_in, WD))
    step("wgu", [], [], lambda: (load("wg", wg_in, WG), load("wu", wu_in, WU)))

    def t_x():
        def body(r, _):
            for c in range(NC):
                v = X[pl.ds(4 * r, 4), :, 16 * c:16 * c + 16, :].reshape(128, D)
                XT[:, pl.ds(pl.multiple_of(256 * c + r * 128, 128), 128)] = v.T
            return 0

        lax.fori_loop(0, 2, body, 0)
        store(XT, xt_out)

    def t_dy():
        def body(r, _):
            DYT[:, pl.ds(pl.multiple_of(r * 128, 128), 128)] = DY[r].reshape(128, D).T
            return 0

        lax.fori_loop(0, 8, body, 0)

    step("tx", x_ends, [], t_x)
    step("tdy", dy_ends, [], t_dy)

    gu_ends = g_ends + u_ends
    n_down = 7 if F % 7 == 0 else 1
    fd = F // n_down

    def down_part(n):
        s = slice(fd * n, fd * (n + 1))

        def body(j, _):
            g = G[pl.ds(8 * j, 8), :, s].astype(F32)
            act = g * (0.5 * jnp.tanh(0.5 * g) + 0.5)
            v = (act * U[pl.ds(8 * j, 8), :, s].astype(F32)).astype(BF)
            HT[pl.ds(2 * j, 2)] = v.reshape(2, 64, fd)
            return 0

        lax.fori_loop(0, 8, body, 0)
        WD[:, s] = jnp.dot(DYT[...], HT[...].reshape(1024, fd), preferred_element_type=F32).astype(BF)
        if n == n_down - 1:
            store(WD, dw_out)

    for n in range(n_down):
        before = [f"down{n - 1}"] if n else ["tdy"] + [f"h{c}m" for c in range(NC)]
        step(f"down{n}", gu_ends, before, lambda n=n: down_part(n))

    def chunk(c):
        nm = f"h{c}"

        def mm_h():
            a = DY[:, :, 16 * c:16 * c + 16, :].reshape(256, D)
            HP[c] = jnp.dot(a, WD[...], preferred_element_type=F32).astype(BF).reshape(16, 16, F)
            send(nm + "rx", HP.at[c, pl.ds(8 * oh, 8)], RX.at[c], p_x)

        def own_sum(zz, k):
            return HP[c, 8 * h + 2 * zz + k].astype(F32) + RX[c, 2 * zz + k].astype(F32)

        def st_a():
            SZ[c, 0, 0] = own_sum(z2, 0).astype(BF)
            send(nm + "rz0", SZ.at[c, 0, 0], RZ.at[c, 0], p_zm)
            SZ[c, 0, 1] = own_sum(z2, 1).astype(BF)
            send(nm + "rz1", SZ.at[c, 0, 1], RZ.at[c, 1], p_zp)
            SZ[c, 1, 0] = own_sum(z1, 0).astype(BF)
            send(nm + "rf00", SZ.at[c, 1, 0], RF.at[c, 0, 0], p_zp)
            SZ[c, 2, 1] = own_sum(z3, 1).astype(BF)
            send(nm + "rf11", SZ.at[c, 2, 1], RF.at[c, 1, 1], p_zm)

        def st_b1():
            SZ[c, 1, 1] = (own_sum(z1, 1) + RZ[c, 1].astype(F32)).astype(BF)
            send(nm + "rf01", SZ.at[c, 1, 1], RF.at[c, 0, 1], p_zp)

        def st_b0():
            SZ[c, 2, 0] = (own_sum(z3, 0) + RZ[c, 0].astype(F32)).astype(BF)
            send(nm + "rf10", SZ.at[c, 2, 0], RF.at[c, 1, 0], p_zm)

        def st_c():
            for k in range(2):
                H[c, 2 * row + k] = (
                    own_sum(z, k) + RF[c, 0, k].astype(F32) + RF[c, 1, k].astype(F32)
                ).astype(BF)

        def st_f():
            def body(j, _):
                g = G[4 * j + c].astype(F32)
                u = U[4 * j + c].astype(F32)
                hh = H[c, j].astype(F32)
                s = 0.5 * jnp.tanh(0.5 * g) + 0.5
                GA[c, j] = (hh * u * s * (1.0 + g * (1.0 - s))).astype(BF)
                UA[c, j] = (hh * g * s).astype(BF)
                return 0

            lax.fori_loop(0, 16, body, 0)
            store(GA.at[c], ga_out.at[c])
            store(UA.at[c], ua_out.at[c])

        def st_g():
            dims = (((1,), (1,)), ((), ()))
            v = lax.dot_general(GA[c].reshape(256, F), WG[...], dims, preferred_element_type=F32)
            v += lax.dot_general(UA[c].reshape(256, F), WU[...], dims, preferred_element_type=F32)
            IGP[c] = v.reshape(8, 2, 16, D)
            send(nm + "c", IGP.at[c, :, oc], RC.at[c], p_s)

        def st_i():
            for xx in range(2):
                for yy in range(4):
                    m = xx * 4 + yy
                    IS[c, yy, xx] = (IGP[c, m, core] + RC[c, m]).astype(BF)
            for i, (yy, p) in enumerate(((y1, p_yp), (y3, p_ym), (y2, p_y2))):
                send(nm + f"y{i}", IS.at[c, yy], RY.at[c, i], p)

        def y_sum(xx):
            v = IS[c, y, xx].astype(F32)
            for i in range(3):
                v += RY[c, i, xx].astype(F32)
            return v

        def st_j():
            IX[c] = y_sum(oxl).astype(BF)
            send(nm + "l", IX.at[c], RL.at[c], p_xl)

        def st_k():
            out[16 * c:16 * c + 16, :] = (y_sum(xl) + RL[c].astype(F32)).astype(BF)

        step(nm + "m", dy_ends + ["wd"], [], mm_h)
        step(nm + "a", [nm + "rx"], [], st_a)
        step(nm + "b1", [nm + "rz1"], [], st_b1)
        step(nm + "b0", [nm + "rz0"], [], st_b0)
        ends = row_gather(
            nm, H.at[c], 2, K1_H[c], first=st_c, after=([nm + k for k in ("rf00", "rf11", "rf01", "rf10")], [])
        )
        step(nm + "f", gu_ends + ends, [], st_f)
        step(nm + "g", ["wg", "wu"], [nm + "f"], st_g)
        step(nm + "i", [nm + "c"], [], st_i)
        step(nm + "j", [nm + f"y{i}" for i in range(3)], [], st_j)
        step(nm + "k", [nm + "l"], [], st_k)

    for c in range(NC):
        chunk(c)

    def gate_part(n):
        r = slice(n * D // 4, (n + 1) * D // 4)
        v = jnp.dot(XT[r, :], GA[...].reshape(1024, F), preferred_element_type=F32)
        OG[r, :] = v.astype(BF)
        store(OG.at[r], gw_out.at[r])

    for n in range(2):
        step(f"w{n}", [], ["tx"] + [f"h{c}f" for c in range(NC)], lambda n=n: gate_part(n))
    run_steps(steps, wait)

    for name in msgs:
        assert name in waited
        wait_send(name)
    for cp in stores:
        cp.wait()


def grads_kernel(
    xt, ua, ga, gw, dw, ig, ou, og, od, oi, XT, UA, GA, OG, DW, OU, IG, isem, osem
):
    D = XT.shape[0]
    rows = D // 4

    def blk(ref, m):
        return ref.at[pl.ds(pl.multiple_of(m * rows, rows), rows)]

    def xt_in(m):
        return pltpu.make_async_copy(blk(xt, m), blk(XT, m), isem.at[m])

    def out(src, dst, m, first):
        return pltpu.make_async_copy(blk(src, m), blk(dst, m), osem.at[first + m])

    top = pl.ds(0, 2 * rows)
    ua_in = pltpu.make_async_copy(ua, UA, isem.at[4])
    ga_in = pltpu.make_async_copy(ga, GA, isem.at[5])
    gw_in = pltpu.make_async_copy(gw, OG.at[top], isem.at[6])
    dw_in = pltpu.make_async_copy(dw, DW, isem.at[7])
    ig_in = pltpu.make_async_copy(ig, IG, isem.at[8])
    gw_out = pltpu.make_async_copy(OG.at[top], og.at[top], osem.at[0])
    dw_out = pltpu.make_async_copy(DW, od, osem.at[1])
    ig_out = pltpu.make_async_copy(IG, oi, osem.at[8])
    xt_in(0).start()
    ua_in.start()
    gw_in.start()
    for m in range(1, 4):
        xt_in(m).start()
    dw_in.start()
    ga_in.start()
    ig_in.start()
    ua_in.wait()

    def up(m, _):
        xt_in(m).wait()
        b = pl.ds(pl.multiple_of(m * rows, rows), rows)
        OU[b, :] = jnp.dot(XT[b, :], UA[...], preferred_element_type=F32).astype(BF)
        out(OU, ou, m, 4).start()
        return 0

    def gate(m, _):
        b = pl.ds(pl.multiple_of(m * rows, rows), rows)
        OG[b, :] = jnp.dot(XT[b, :], GA[...], preferred_element_type=F32).astype(BF)
        out(OG, og, m, 0).start()
        return 0

    lax.fori_loop(0, 1, up, 0)
    gw_in.wait()
    gw_out.start()
    lax.fori_loop(1, 2, up, 0)
    dw_in.wait()
    dw_out.start()
    ig_in.wait()
    ig_out.start()
    lax.fori_loop(2, 4, up, 0)
    ga_in.wait()
    lax.fori_loop(2, 4, gate, 0)
    for m in range(4):
        out(OU, ou, m, 4).wait()
    for m in range(2, 4):
        out(OG, og, m, 0).wait()
    gw_out.wait()
    dw_out.wait()
    ig_out.wait()


def on_device(inputs, out_grad, gate_pre, up_pre, gate_weight, up_weight, down_weight):
    D, F = gate_weight.shape
    T = 1024
    any_spec = pl.BlockSpec(memory_space=pl.ANY)
    v = pltpu.VMEM
    scratch = [
        v((8, 2, 64, D), BF), v((8, 2, 64, D), BF),
        v((64, 16, F), BF), v((64, 16, F), BF),
        v((D, F), BF), v((D, F), BF), v((D, F), BF),
        v((NC, 16, 16, F), BF), v((NC, 8, 16, F), BF),
        v((NC, 3, 2, 16, F), BF), v((NC, 2, 16, F), BF), v((NC, 2, 2, 16, F), BF),
        v((NC, 16, 16, F), BF),
        v((NC, 16, 16, F), BF), v((NC, 16, 16, F), BF),
        v((16, 64, F // 7 if F % 7 == 0 else F), BF),
        v((D, T), BF), v((D, T), BF), v((D // 2, F), BF),
        v((NC, 8, 2, 16, D), F32), v((NC, 8, 16, D), F32),
        v((NC, 4, 2, 16, D), BF), v((NC, 3, 2, 16, D), BF),
        v((NC, 16, D), BF), v((NC, 16, D), BF),
        pltpu.SemaphoreType.DMA((N_MSG,)), pltpu.SemaphoreType.DMA((N_MSG,)), pltpu.SemaphoreType.DMA((32,)),
    ]
    sd = jax.ShapeDtypeStruct
    input_grad, gw, ga, ua, xt, dw = pl.pallas_call(
        comm_kernel,
        out_shape=(
            sd((64, D), BF), sd((D // 2, F), BF), sd((NC, 16, 16, F), BF), sd((NC, 16, 16, F), BF),
            sd((D, T), BF), sd((D, F), BF),
        ),
        in_specs=[any_spec] * 7,
        out_specs=(pl.BlockSpec(memory_space=pltpu.VMEM),) + (any_spec,) * 5,
        scratch_shapes=scratch,
        compiler_params=pltpu.CompilerParams(
            collective_id=0, has_side_effects=True, vmem_limit_bytes=VMEM_LIMIT
        ),
        cost_estimate=pl.CostEstimate(flops=9 * D * F * T, bytes_accessed=30 << 20, transcendentals=T * F),
        name="comm",
    )(
        inputs, out_grad, gate_pre.reshape(8, 16, F), up_pre.reshape(8, 16, F),
        gate_weight, up_weight, down_weight,
    )
    uw, gw, dw, input_grad = pl.pallas_call(
        grads_kernel,
        out_shape=(sd((D, F), BF),) * 3 + (sd((64, D), BF),),
        in_specs=[any_spec] * 6,
        out_specs=(any_spec,) * 4,
        scratch_shapes=[
            v((D, T), BF), v((T, F), BF), v((T, F), BF), v((D, F), BF), v((D, F), BF), v((D, F), BF),
            v((64, D), BF), pltpu.SemaphoreType.DMA((9,)), pltpu.SemaphoreType.DMA((9,)),
        ],
        compiler_params=pltpu.CompilerParams(vmem_limit_bytes=VMEM_LIMIT),
        cost_estimate=pl.CostEstimate(flops=3 * D * F * T, bytes_accessed=26 << 20, transcendentals=0),
        name="weight_grads",
    )(xt, ua.reshape(T, F), ga.reshape(T, F), gw, dw, input_grad)
    return input_grad, gw, uw, dw


def solution(mesh):
    in_specs = (P("col", "row"), P("col", "row")) + (P("row", "col"),) * 5
    out_specs = (P("col", "row"), P("row", "col"), P("row", "col"), P("row", "col"))
    return jax.shard_map(
        on_device, mesh=mesh, in_specs=in_specs, out_specs=out_specs, check_vma=False
    )
```
